32 devices in a mesh: row: 16 (over z, x, core), col: 2 (over y).
Axes of the slice: x: 2, y: 2, z: 4, core: 2. Of those that a mesh axis runs over, the one named last changes fastest.
Arguments:
- positions: float32 [3, 131072], P(None, ('row', 'col')), may hold values from 0 to 385, as said below
- atom_type: int32 [131072], P(('row', 'col')), may hold values from 0 to 5
- krylov: float32 [16, 131072], P(None, ('row', 'col')), may hold values from -6 to 6
- block_order: int32 [131072], P(('row', 'col')), may hold values from 0 to 4095, as said below
- type_width: float32 [6], replicated, may hold values from 0.5 to 2.5
- type_hard: float32 [6], replicated, may hold values from 1 to 4
- pair_rows: int32 [16, 2, 512], P('row', 'col'), may hold values from 0 to 63, as said below
- pair_cols: int32 [16, 2, 512], P('row', 'col'), may hold values from 0 to 511, as said below
- pair_count: int32 [16, 2], P('row', 'col'), may hold values from 1 to 512, as said below
Outputs:
- coulomb_response: float32 [16, 131072], P(None, ('row', 'col'))
The draws below stay inside these ranges and needn't reach their ends.
Inputs may be any that keep to these rules, and one draw needn't show every extreme that they name: `positions`: global block g is a cell of a grid with coordinates (g // 64, (g // 32) % 2, g % 32); each atom of block g lies in the box of sides 44, 30 and 44 whose lowest corner is the cell's coordinates times 11, 5 and 11. `block_order`: within each device's shard of 4096 atoms, the entries are a permutation of 0 to 4095. `pair_rows`: in slots below pair_count the pairs (i, j) are distinct, have i <= j, and their grid cells differ by at most 2 along the first and third dimensions and at most 4 along the second; for device (r, c), pair_cols // 32 is r, r + 1 or r + 2 there. Other slots hold indices in range that are not used. `pair_cols`: see pair_rows. `pair_count`: some device's list is full.
All inputs are finite; a program needn't handle non-finite values.
Results may differ from the reference program's by a relative error of at most 0.00665.
Values may be sent and summed in bfloat16 or wider, within the bound.
A program may use at most 128 MiB of HBM per device.

```python
import math
import jax
import jax.numpy as jnp
from jax import lax

VECS = 16
BLK = 128
NTYPES = 6
BLOCKS_DEV = 32
PAIRS_DEV = 512
ATOMS = 131072
N_ROW = 16
N_COL = 2


def block_orders(key):
    shard_keys = jax.random.split(jax.random.fold_in(key, 29), N_ROW * N_COL)

    def one_shard(shard_key):
        return jax.random.permutation(shard_key, BLOCKS_DEV * BLK).astype(jnp.int32)
    return jax.vmap(one_shard)(shard_keys)


def draw_block_order(key, part):
    return block_orders(key).reshape(-1)


def draw_positions(key, part):
    orders = block_orders(key)
    shard_atoms = BLOCKS_DEV * BLK
    atom_total = N_ROW * N_COL * shard_atoms
    blocked = jnp.arange(atom_total, dtype=jnp.int32)
    global_block = blocked // BLK
    cell_z = global_block % BLOCKS_DEV
    cell_y = global_block // BLOCKS_DEV % N_COL
    cell_x = global_block // (BLOCKS_DEV * N_COL)
    cells = jnp.stack([cell_x, cell_y, cell_z]).astype(jnp.float32)
    jitter = jax.random.uniform(jax.random.fold_in(key, 41), (3, atom_total), jnp.float32, 0.0, 0.999)
    spacing = jnp.array([11.0, 5.0, 11.0], jnp.float32)[:, None]
    extent = jnp.array([44.0, 30.0, 44.0], jnp.float32)[:, None]
    values = spacing * cells + extent * jitter
    atom_index = (blocked // shard_atoms * shard_atoms + orders.reshape(-1)).astype(jnp.int32)
    return jnp.zeros((3, atom_total), jnp.float32).at[:, atom_index].set(values)


def pair_lists(key):
    device_total = N_ROW * N_COL
    device_keys = jax.random.split(jax.random.fold_in(key, 11), device_total)
    row_blocks = N_COL * BLOCKS_DEV
    candidates = 3 * row_blocks * BLOCKS_DEV
    full_device = min(2, N_COL - 1)

    def one_device(device_key, device):
        row_index = device // N_COL
        col_index = device % N_COL
        shuffled = jax.random.permutation(device_key, candidates).astype(jnp.int32)
        local_row = shuffled % row_blocks
        rest = shuffled // row_blocks
        col_z = rest % BLOCKS_DEV
        step_x = rest // BLOCKS_DEV
        col_slab = row_index + step_x
        row_y = local_row // BLOCKS_DEV
        row_z = local_row % BLOCKS_DEV
        near = (jnp.abs(row_y - col_index) <= 4) & (jnp.abs(row_z - col_z) <= 2) & (col_slab < N_ROW)
        upper = (step_x > 0) | (col_index * BLOCKS_DEV + col_z >= local_row)
        valid = (near & upper).astype(jnp.int32)
        local_col = jnp.minimum(col_slab * BLOCKS_DEV + col_z, N_ROW * BLOCKS_DEV - 1).astype(jnp.int32)
        scores = (1 - valid) * candidates + jnp.arange(candidates, dtype=jnp.int32)
        picked = jnp.argsort(scores)[:PAIRS_DEV]
        wanted = jax.random.randint(jax.random.fold_in(device_key, 3), (), PAIRS_DEV // 4, PAIRS_DEV + 1)
        wanted = jnp.where(device == full_device, PAIRS_DEV, wanted)
        live_count = jnp.minimum(wanted, jnp.sum(valid)).astype(jnp.int32)
        return (local_row[picked], local_col[picked], live_count)
    rows_all, cols_all, counts_all = jax.vmap(one_device)(device_keys, jnp.arange(device_total, dtype=jnp.int32))
    return (rows_all.reshape(N_ROW, N_COL, PAIRS_DEV), cols_all.reshape(N_ROW, N_COL, PAIRS_DEV), counts_all.reshape(N_ROW, N_COL))


def draw_pair_rows(key, part):
    return pair_lists(key)[0]


def draw_pair_cols(key, part):
    return pair_lists(key)[1]


def draw_pair_count(key, part):
    return pair_lists(key)[2]


def touch_ends(values, own_key, low, high):
    place = [jax.random.randint(jax.random.fold_in(own_key, axis), (), 0, length) for axis, length in enumerate(values.shape)]
    widest = values.shape.index(max(values.shape))
    neighbour = place[:widest] + [(place[widest] + 1) % values.shape[widest]] + place[widest + 1:]
    return values.at[tuple(place)].set(low).at[tuple(neighbour)].set(high)


def levels(stream_key, dims, cuts, low, high):
    gain = 1.0
    for position, blocks in cuts:
        heights = jax.random.uniform(jax.random.fold_in(jax.random.fold_in(stream_key, 6), position), (blocks,), jnp.float32, low / len(cuts), high / len(cuts))
        gain = gain * jnp.repeat(jnp.exp(heights), dims[position] // blocks).reshape((-1,) + (1,) * (len(dims) - 1 - position))
    return gain


def normal_values(rng, shape, scale, reach, shards=(), kind=jnp.bfloat16):
    gain = levels(rng, shape, shards, -0.22, 0.18) if shards else 1.0
    values = jax.random.normal(rng, shape, jnp.float32) * scale * gain
    return jnp.minimum(jnp.maximum(values, -reach), reach).astype(kind)


def setup_inputs(seed: int = 0) -> dict:
    keys = jax.random.split(jax.random.key(seed), 10)
    positions = draw_positions(jax.random.fold_in(keys[9], 71), 0)
    atom_type = touch_ends(jax.random.randint(keys[1], (ATOMS,), 0, NTYPES), jax.random.fold_in(keys[1], 1), 0, NTYPES - 1).astype(jnp.int32)
    krylov = normal_values(keys[2], (VECS, ATOMS), 1.0, 6.0, ((1, 32),), jnp.float32)
    block_order = draw_block_order(jax.random.fold_in(keys[9], 71), 0)
    type_width = jnp.clip(jnp.exp(jax.random.uniform(keys[4], (NTYPES,), jnp.float32, math.log(0.5), math.log(2.5))), 0.5, 2.5)
    type_hard = jnp.clip(jax.random.uniform(keys[5], (NTYPES,), jnp.float32, 1.0, 4.0), 1.0, 4.0)
    pair_rows = draw_pair_rows(jax.random.fold_in(keys[9], 71), 0)
    pair_cols = draw_pair_cols(jax.random.fold_in(keys[9], 71), 0)
    pair_count = draw_pair_count(jax.random.fold_in(keys[9], 71), 0)
    return dict(positions=positions, atom_type=atom_type, krylov=krylov, block_order=block_order, type_width=type_width, type_hard=type_hard, pair_rows=pair_rows, pair_cols=pair_cols, pair_count=pair_count)


SOFTENING = 0.5

def kernel_tiles(left_geometry, right_geometry):
    offsets = left_geometry[:, 0:3, :, None] - right_geometry[:, 0:3, None, :]
    distance = jnp.sqrt(lax.optimization_barrier(jnp.sum(offsets * offsets, axis=1)) + SOFTENING * SOFTENING)
    spread = left_geometry[:, 3, :, None] ** 2 + right_geometry[:, 3, None, :] ** 2
    return (lax.erf(distance * lax.rsqrt(spread)) / distance).astype(jnp.bfloat16)

def reference(positions, atom_type, krylov, block_order, type_width, type_hard, pair_rows, pair_cols, pair_count):
    atom_total = positions.shape[1]
    shard_atoms = BLOCKS_DEV * BLK
    blocks_all = atom_total // BLK
    offsets = jnp.arange(atom_total, dtype=jnp.int32) // shard_atoms * shard_atoms
    ordering = (offsets + block_order).astype(jnp.int32)
    widths = type_width[atom_type]
    hardness = type_hard[atom_type]
    geometry = jnp.concatenate([positions, widths[None, :]], axis=0)[:, ordering]
    vectors = krylov.astype(jnp.bfloat16)[:, ordering]
    geometry_blocks = geometry.reshape(4, blocks_all, BLK).transpose(1, 0, 2)
    vector_blocks = vectors.reshape(VECS, blocks_all, BLK).transpose(1, 0, 2)
    row_ids = jnp.arange(N_ROW, dtype=jnp.int32)[:, None, None]
    col_ids = jnp.arange(N_COL, dtype=jnp.int32)[None, :, None]
    row_global = (row_ids * (N_COL * BLOCKS_DEV) + pair_rows).astype(jnp.int32)
    col_global = ((pair_cols // BLOCKS_DEV * N_COL + col_ids) * BLOCKS_DEV + pair_cols % BLOCKS_DEV).astype(jnp.int32)
    slot_index = jnp.arange(PAIRS_DEV, dtype=jnp.int32)[None, None, :]
    live_flags = (slot_index < pair_count[:, :, None]).astype(jnp.float32)
    pair_total = N_ROW * N_COL * PAIRS_DEV
    batch_rows = math.gcd(pair_total, 256)
    row_global = row_global.reshape(-1, batch_rows)
    col_global = col_global.reshape(-1, batch_rows)
    live_flags = live_flags.reshape(-1, batch_rows)

    def pair_step(accumulated, pair_items):
        left_block, right_block, alive_now = pair_items
        tiles_now = kernel_tiles(geometry_blocks[left_block], geometry_blocks[right_block]).astype(jnp.float32)
        left_vectors = vector_blocks[left_block].astype(jnp.float32)
        right_vectors = vector_blocks[right_block].astype(jnp.float32)
        forward = jnp.einsum('pab,pvb->pva', tiles_now, right_vectors) * alive_now[:, None, None]
        mirror = alive_now * (left_block != right_block).astype(jnp.float32)
        backward = jnp.einsum('pab,pva->pvb', tiles_now, left_vectors) * mirror[:, None, None]
        accumulated = accumulated.at[left_block].add(forward).at[right_block].add(backward)
        return (accumulated, None)
    initial = jnp.zeros((blocks_all, VECS, BLK), jnp.float32)
    summed, _ = lax.scan(pair_step, initial, (row_global, col_global, live_flags))
    blocked = summed.transpose(1, 0, 2).reshape(VECS, atom_total)
    result = jnp.zeros((VECS, atom_total), jnp.float32).at[:, ordering].set(blocked)
    return result + hardness[None, :] * krylov
```

```python
import functools

import jax
import jax.numpy as jnp
from jax import lax
from jax.experimental import pallas as pl
from jax.experimental.pallas import tpu as pltpu
from jax.sharding import PartitionSpec as P

BLK = 128
SOFTENING = 0.5
UNROLL = 4
CHUNK = 32
VMEM_BYTES = 56 * 1024 * 1024
ERF_POLY = (
    1.1283793236455961,
    0.10276865621773908,
    -0.00019100361666571117,
    -0.0006204428648261939,
    8.78674655970463e-05,
    -5.703654839853857e-06,
    1.4374848121852195e-07,
)


def split3(values):
    high = values.astype(jnp.bfloat16).astype(jnp.float32)
    rest = values - high
    mid = rest.astype(jnp.bfloat16).astype(jnp.float32)
    low = (rest - mid).astype(jnp.bfloat16).astype(jnp.float32)
    return high, mid, low


def gather_kernel(place_ref, type_ref, krylov_ref, order_ref, geometry_ref, vectors_ref, stacked_ref):
    atoms = place_ref.shape[1]
    vecs = krylov_ref.shape[0]
    groups = atoms // BLK
    rows = 16 + vecs
    width = order_ref.shape[1]

    @pl.when(pl.program_id(0) == 0)
    def _():
        high, mid, low = split3(place_ref[...])
        kinds = type_ref[...].astype(jnp.float32)
        empty = jnp.zeros((6, atoms), jnp.float32)
        full = jnp.concatenate([high, mid, low, kinds, empty, krylov_ref[...]], axis=0).astype(jnp.bfloat16)
        for group in range(groups):
            stacked_ref[group * rows : (group + 1) * rows] = full[:, group * BLK : (group + 1) * BLK]

    order = order_ref[...]
    group_of, lane_of = order // BLK, order % BLK
    lane_ids = lax.broadcasted_iota(jnp.int32, (BLK, width), 0)
    picked = (lane_ids == lane_of).astype(jnp.float32).astype(jnp.bfloat16)
    total = jnp.zeros((rows, width), jnp.float32)
    for group in range(groups):
        here = jnp.dot(
            stacked_ref[group * rows : (group + 1) * rows], picked, preferred_element_type=jnp.float32
        )
        total = jnp.where(group_of == group, here, total)
    place = total[0:3] + total[3:6] + total[6:9]
    geometry_ref[...] = jnp.concatenate([place, total[9:10], jnp.zeros((4, width), jnp.float32)], axis=0)
    vectors_ref[...] = total[16:].astype(jnp.bfloat16)


def gathered(positions, atom_type, krylov, order, tile=512):
    vecs, atoms = krylov.shape
    return pl.pallas_call(
        gather_kernel,
        grid=(atoms // tile,),
        in_specs=[
            pl.BlockSpec((3, atoms), lambda step: (0, 0)),
            pl.BlockSpec((1, atoms), lambda step: (0, 0)),
            pl.BlockSpec((vecs, atoms), lambda step: (0, 0)),
            pl.BlockSpec((1, tile), lambda step: (0, step)),
        ],
        out_specs=[
            pl.BlockSpec((8, tile), lambda step: (0, step)),
            pl.BlockSpec((vecs, tile), lambda step: (0, step)),
        ],
        out_shape=[
            jax.ShapeDtypeStruct((8, atoms), jnp.float32),
            jax.ShapeDtypeStruct((vecs, atoms), jnp.bfloat16),
        ],
        scratch_shapes=[pltpu.VMEM((atoms // BLK * (16 + vecs), BLK), jnp.bfloat16)],
        compiler_params=pltpu.CompilerParams(vmem_limit_bytes=VMEM_BYTES),
        cost_estimate=pl.CostEstimate(
            flops=2 * (16 + vecs) * atoms * atoms, bytes_accessed=8 * vecs * atoms, transcendentals=0
        ),
        name="gather_atoms",
    )(positions, atom_type[None, :], krylov, order[None, :])


def scatter_kernel(order_ref, krylov_ref, type_ref, hard_ref, *refs):
    parts, (out_ref, split_ref) = refs[:-2], refs[-2:]
    vecs, atoms = krylov_ref.shape
    groups = atoms // BLK
    chunk = 512
    total = parts[0][...]
    for part in parts[1:]:
        total = total + part[...].astype(jnp.float32)
    high = total.astype(jnp.bfloat16).astype(jnp.float32)
    split_ref[0:vecs] = high
    split_ref[vecs:] = total - high

    lane_ids = lax.broadcasted_iota(jnp.int32, (BLK, chunk), 0)

    def chunk_step(step, total):
        lanes = pl.ds(pl.multiple_of(step * chunk, chunk), chunk)
        order = order_ref[:, lanes]
        group_of, lane_of = order // BLK, order % BLK
        placed = (lane_ids == lane_of).astype(jnp.float32).astype(jnp.bfloat16)
        values = split_ref[:, lanes]
        masked = jnp.concatenate(
            [jnp.where(group_of == group, values, 0.0).astype(jnp.bfloat16) for group in range(groups)], axis=0
        )
        return total + lax.dot_general(
            masked, placed, (((1,), (1,)), ((), ())), preferred_element_type=jnp.float32
        )

    moved = lax.fori_loop(
        0, atoms // chunk, chunk_step, jnp.zeros((groups * 2 * vecs, BLK), jnp.float32)
    )
    kinds = type_ref[...]
    hardness = jnp.zeros((1, atoms), jnp.float32)
    for kind in range(hard_ref.shape[0]):
        hardness = jnp.where(kinds == kind, hard_ref[kind], hardness)
    for group in range(groups):
        lanes = slice(group * BLK, (group + 1) * BLK)
        first = group * 2 * vecs
        placed = moved[first : first + vecs] + moved[first + vecs : first + 2 * vecs]
        out_ref[:, lanes] = placed + hardness[:, lanes] * krylov_ref[:, lanes]


def scattered(order, krylov, atom_type, type_hard, parts):
    vecs, atoms = krylov.shape
    vmem = pl.BlockSpec(memory_space=pltpu.VMEM)
    return pl.pallas_call(
        scatter_kernel,
        in_specs=[vmem] * 3 + [pl.BlockSpec(memory_space=pltpu.SMEM)] + [vmem] * len(parts),
        out_specs=vmem,
        out_shape=jax.ShapeDtypeStruct((vecs, atoms), jnp.float32),
        scratch_shapes=[pltpu.VMEM((2 * vecs, atoms), jnp.float32)],
        compiler_params=pltpu.CompilerParams(vmem_limit_bytes=VMEM_BYTES),
        cost_estimate=pl.CostEstimate(
            flops=4 * vecs * atoms * atoms, bytes_accessed=24 * vecs * atoms, transcendentals=0
        ),
        name="scatter_atoms",
    )(order[None, :], krylov, atom_type[None, :], type_hard, *parts)


def lanes_of(block):
    return pl.ds(pl.multiple_of(block * BLK, BLK), BLK)


def pair_kernel(slabs, left_blocks, left_ids, right_ids, count_ref, table_ref, *refs):
    geo_refs, vec_refs = refs[:slabs], refs[slabs : 2 * slabs]
    out_refs = refs[2 * slabs : 3 * slabs]
    left_ref, origin_ref, geo_ref, mix_ref, vec_ref, acc_ref, both_ref, tile_ref = refs[3 * slabs :]
    atoms = geo_refs[0].shape[1]
    blocks = slabs * atoms // BLK
    row_id = lax.broadcasted_iota(jnp.int32, (8, BLK), 0)
    type_width = table_ref[...]

    for slab in range(slabs):
        geo_ref[:, slab * atoms : (slab + 1) * atoms] = geo_refs[slab][...]
        vec_ref[:, slab * atoms : (slab + 1) * atoms] = vec_refs[slab][...]
    acc_ref[...] = jnp.zeros_like(acc_ref)

    def one_hot(geometry):
        return jnp.where(row_id.astype(jnp.float32) == geometry[3:4, :], 1.0, 0.0)

    def mix_step(block, carry):
        hot = one_hot(geo_ref[:, lanes_of(block)])
        width = jnp.sum(hot * type_width, axis=0, keepdims=True)
        high, mid, low = split3(lax.rsqrt(type_width * type_width + width * width))
        mix_ref[:, lanes_of(block)] = jnp.concatenate([high, mid, low, jnp.zeros_like(low)], axis=0).astype(
            jnp.bfloat16
        )
        return carry

    lax.fori_loop(0, blocks, mix_step, 0)

    def left_step(block, carry):
        geometry = geo_ref[:, lanes_of(block)]
        hot = one_hot(geometry)
        origin = jnp.broadcast_to(geometry[:, 0:1], (8, BLK))
        origin_ref[block] = origin
        local = jnp.where(row_id < 3, geometry - origin, 0.0)
        norm = jnp.sum(local * local, axis=0, keepdims=True) + SOFTENING * SOFTENING
        side = jnp.where(row_id < 3, -2.0 * local, jnp.where(row_id == 3, 1.0, jnp.where(row_id == 4, norm, 0.0)))
        high, mid, low = split3(side)
        rows = jnp.concatenate(
            [high, high, mid, mid, high, low, hot, hot, hot, jnp.zeros((BLK - 72, BLK), jnp.float32)], axis=0
        )
        left_ref[block] = rows.T.astype(jnp.bfloat16)
        return carry

    lax.fori_loop(0, left_blocks, left_step, 0)

    both_ref[...] = jnp.ones_like(both_ref)
    tile_ref[...] = jnp.zeros_like(tile_ref)
    slots = left_ids.shape[0]
    live = count_ref[0]
    zero_side = jnp.zeros((48, BLK), jnp.bfloat16)
    zero_mix = jnp.zeros((32, BLK), jnp.bfloat16)
    zero_tail = jnp.zeros((BLK - 80, 2 * BLK), jnp.bfloat16)

    def weights_of(left, right):
        geometry = geo_ref[:, lanes_of(right)]
        local = jnp.where(row_id < 3, geometry - origin_ref[left], 0.0)
        norm = jnp.sum(local * local, axis=0, keepdims=True)
        side = jnp.where(row_id == 3, norm, jnp.where(row_id == 4, 1.0, local))
        high, mid, low = split3(side)
        rows = jnp.concatenate([high, mid, high, mid, low, high], axis=0).astype(jnp.bfloat16)
        mix = mix_ref[:, lanes_of(right)]
        return jnp.concatenate(
            [
                jnp.concatenate([rows, zero_side], axis=1),
                jnp.concatenate([zero_mix, mix], axis=1),
                zero_tail,
            ],
            axis=0,
        )

    def screened(square, inverse_width):
        inverse = lax.rsqrt(square)
        scaled = square * inverse * inverse_width
        power = scaled * scaled
        series = jnp.float32(ERF_POLY[-1])
        for factor in ERF_POLY[-2::-1]:
            series = series * power + factor
        return (jnp.tanh(scaled * series) * inverse).astype(jnp.bfloat16)

    def slot_ids(turn, offset):
        slot = turn * UNROLL + offset
        place = jnp.clip(slot, 0, slots - 1)
        return left_ids[place], right_ids[place], (slot >= 0) & (slot < live)

    def pair_step(turn, carry):
        done = []
        for offset in range(UNROLL):
            left, right, alive = slot_ids(turn - 2, offset)
            tile = tile_ref[offset]
            forward = lax.dot_general(
                vec_ref[:, lanes_of(right)], tile, (((1,), (1,)), ((), ())), preferred_element_type=jnp.float32
            )
            backward = jnp.dot(vec_ref[:, lanes_of(left)], tile, preferred_element_type=jnp.float32)
            done.append((left, right, forward, backward, alive))
        for offset in range(UNROLL):
            for first in range(0, BLK, CHUNK):
                rows = slice(first, first + CHUNK)
                tile_ref[offset, rows] = screened(both_ref[offset, rows, :BLK], both_ref[offset, rows, BLK:])
        for offset in range(UNROLL):
            left, right, _ = slot_ids(turn, offset)
            both_ref[offset] = jnp.dot(
                left_ref[left], weights_of(left, right), preferred_element_type=jnp.float32
            )
        for left, right, forward, backward, alive in done:
            acc_ref[:, lanes_of(left)] += jnp.where(alive, forward, 0.0)
            acc_ref[:, lanes_of(right)] += jnp.where(alive & (left != right), backward, 0.0)
        return carry

    lax.fori_loop(0, (live + UNROLL - 1) // UNROLL + 2, pair_step, 0)

    for slab in range(slabs):
        out_refs[slab][...] = acc_ref[:, slab * atoms : (slab + 1) * atoms].astype(out_refs[slab].dtype)


def pair_sums(geometries, vectors, left_ids, right_ids, count, table, left_blocks):
    slabs = len(geometries)
    atoms = geometries[0].shape[1]
    vecs = vectors[0].shape[0]
    smem = pl.BlockSpec(memory_space=pltpu.SMEM)
    vmem = pl.BlockSpec(memory_space=pltpu.VMEM)
    kinds = [jnp.float32] + [jnp.bfloat16] * (slabs - 1)
    return pl.pallas_call(
        functools.partial(pair_kernel, slabs, left_blocks),
        in_specs=[smem] * 3 + [vmem] * (1 + 2 * slabs),
        out_specs=[vmem] * slabs,
        out_shape=[jax.ShapeDtypeStruct((vecs, atoms), kind) for kind in kinds],
        scratch_shapes=[
            pltpu.VMEM((left_blocks, BLK, BLK), jnp.bfloat16),
            pltpu.VMEM((left_blocks, 8, BLK), jnp.float32),
            pltpu.VMEM((8, slabs * atoms), jnp.float32),
            pltpu.VMEM((32, slabs * atoms), jnp.bfloat16),
            pltpu.VMEM((vecs, slabs * atoms), jnp.bfloat16),
            pltpu.VMEM((vecs, slabs * atoms), jnp.float32),
            pltpu.VMEM((UNROLL, BLK, 2 * BLK), jnp.float32),
            pltpu.VMEM((UNROLL, BLK, BLK), jnp.bfloat16),
        ],
        compiler_params=pltpu.CompilerParams(vmem_limit_bytes=VMEM_BYTES),
        cost_estimate=pl.CostEstimate(
            flops=left_ids.shape[0] * BLK * BLK * (4 * vecs + 320),
            bytes_accessed=slabs * atoms * (32 + 4 * vecs),
            transcendentals=2 * left_ids.shape[0] * BLK * BLK,
        ),
        name="pair_sums",
    )(left_ids, right_ids, count, table, *geometries, *vectors)


def along_row(value, steps):
    count = lax.axis_size("row")
    first, last = max(0, -steps), min(count, count - steps)
    return lax.ppermute(value, "row", [(source, source + steps) for source in range(first, last)])


def along_col(value, steps):
    count = lax.axis_size("col")
    return lax.ppermute(value, "col", [(source, (source + steps) % count) for source in range(count)])


def on_device(
    positions, atom_type, krylov, block_order, type_width, type_hard, pair_rows, pair_cols, pair_count
):
    vecs, atoms = krylov.shape
    shard_blocks = atoms // BLK
    geometry, vectors = gathered(positions, atom_type, krylov, block_order)

    col_devices = lax.axis_size("col")
    peers = [("col", step) for step in range(1, col_devices)] + [("row", 1), ("row", 2)]
    moved = {"col": along_col, "row": along_row}
    geometries = [geometry] + [moved[axis](geometry, -step) for axis, step in peers]
    panels = [vectors] + [moved[axis](vectors, -step) for axis, step in peers]

    row_index = lax.axis_index("row")
    col_index = lax.axis_index("col")
    rows_list = pair_rows.reshape(-1)
    cols_list = pair_cols.reshape(-1)
    row_slab = (rows_list // shard_blocks - col_index + col_devices) % col_devices
    left_ids = row_slab * shard_blocks + rows_list % shard_blocks
    step = jnp.clip(cols_list // shard_blocks - row_index, 0, 2)
    right_slab = jnp.where(step == 0, 0, step + col_devices - 1)
    right_ids = right_slab * shard_blocks + cols_list % shard_blocks
    table = jnp.zeros((8, BLK), jnp.float32) + jnp.pad(
        type_width, (0, 8 - type_width.shape[0]), constant_values=1.0
    )[:, None]
    sums = pair_sums(
        geometries, panels, left_ids, right_ids, pair_count.reshape(1), table, col_devices * shard_blocks
    )
    returned = [sums[0]] + [moved[axis](part, step) for (axis, step), part in zip(peers, sums[1:])]
    return scattered(block_order, krylov, atom_type, type_hard, returned)


def solution(mesh):
    placed = (
        P(None, ("row", "col")),
        P(("row", "col")),
        P(None, ("row", "col")),
        P(("row", "col")),
        P(),
        P(),
        P("row", "col", None),
        P("row", "col", None),
        P("row", "col"),
    )
    return jax.shard_map(
        on_device, mesh=mesh, in_specs=placed, out_specs=P(None, ("row", "col")), check_vma=False
    )
```

```python
import functools

import jax
import jax.numpy as jnp
from jax import lax
from jax.experimental import pallas as pl
from jax.experimental.pallas import tpu as pltpu
from jax.sharding import PartitionSpec as P

BLK = 128
SOFTENING = 0.5
UNROLL = 4
CHUNK = 32
VMEM_BYTES = 56 * 1024 * 1024
SLOPE = 1.1283737853323306
ERF_SERIES = (
    0.07159415430567773,
    -0.00022649025157034893,
    -0.000190667906232071,
    1.1875337467865749e-05,
)


def split3(values):
    high = values.astype(jnp.bfloat16).astype(jnp.float32)
    rest = values - high
    mid = rest.astype(jnp.bfloat16).astype(jnp.float32)
    low = (rest - mid).astype(jnp.bfloat16).astype(jnp.float32)
    return high, mid, low


def gather_kernel(place_ref, type_ref, krylov_ref, order_ref, geometry_ref, vectors_ref, stacked_ref):
    atoms = place_ref.shape[1]
    vecs = krylov_ref.shape[0]
    groups = atoms // BLK
    rows = 16 + vecs
    width = order_ref.shape[1]

    @pl.when(pl.program_id(0) == 0)
    def _():
        high, mid, low = split3(place_ref[...])
        kinds = type_ref[...].astype(jnp.float32)
        empty = jnp.zeros((6, atoms), jnp.float32)
        full = jnp.concatenate([high, mid, low, kinds, empty, krylov_ref[...]], axis=0).astype(jnp.bfloat16)
        for group in range(groups):
            stacked_ref[group * rows : (group + 1) * rows] = full[:, group * BLK : (group + 1) * BLK]

    order = order_ref[...]
    group_of, lane_of = order // BLK, order % BLK
    lane_ids = lax.broadcasted_iota(jnp.int32, (BLK, width), 0)
    picked = (lane_ids == lane_of).astype(jnp.float32).astype(jnp.bfloat16)
    total = jnp.zeros((rows, width), jnp.float32)
    for group in range(groups):
        here = jnp.dot(
            stacked_ref[group * rows : (group + 1) * rows], picked, preferred_element_type=jnp.float32
        )
        total = jnp.where(group_of == group, here, total)
    place = total[0:3] + total[3:6] + total[6:9]
    geometry_ref[...] = jnp.concatenate([place, total[9:10], jnp.zeros((4, width), jnp.float32)], axis=0)
    vectors_ref[...] = total[16:].astype(jnp.bfloat16)


def gathered(positions, atom_type, krylov, order, tile=512):
    vecs, atoms = krylov.shape
    return pl.pallas_call(
        gather_kernel,
        grid=(atoms // tile,),
        in_specs=[
            pl.BlockSpec((3, atoms), lambda step: (0, 0)),
            pl.BlockSpec((1, atoms), lambda step: (0, 0)),
            pl.BlockSpec((vecs, atoms), lambda step: (0, 0)),
            pl.BlockSpec((1, tile), lambda step: (0, step)),
        ],
        out_specs=[
            pl.BlockSpec((8, tile), lambda step: (0, step)),
            pl.BlockSpec((vecs, tile), lambda step: (0, step)),
        ],
        out_shape=[
            jax.ShapeDtypeStruct((8, atoms), jnp.float32),
            jax.ShapeDtypeStruct((vecs, atoms), jnp.bfloat16),
        ],
        scratch_shapes=[pltpu.VMEM((atoms // BLK * (16 + vecs), BLK), jnp.bfloat16)],
        compiler_params=pltpu.CompilerParams(vmem_limit_bytes=VMEM_BYTES),
        cost_estimate=pl.CostEstimate(
            flops=2 * (16 + vecs) * atoms * atoms, bytes_accessed=8 * vecs * atoms, transcendentals=0
        ),
        name="gather_atoms",
    )(positions, atom_type[None, :], krylov, order[None, :])


def scatter_kernel(order_ref, krylov_ref, type_ref, hard_ref, *refs):
    parts, (out_ref, split_ref) = refs[:-2], refs[-2:]
    vecs, atoms = krylov_ref.shape
    groups = atoms // BLK
    chunk = 512
    total = parts[0][...]
    for part in parts[1:]:
        total = total + part[...].astype(jnp.float32)
    high = total.astype(jnp.bfloat16).astype(jnp.float32)
    split_ref[0:vecs] = high
    split_ref[vecs:] = total - high

    lane_ids = lax.broadcasted_iota(jnp.int32, (BLK, chunk), 0)

    def chunk_step(step, total):
        lanes = pl.ds(pl.multiple_of(step * chunk, chunk), chunk)
        order = order_ref[:, lanes]
        group_of, lane_of = order // BLK, order % BLK
        placed = (lane_ids == lane_of).astype(jnp.float32).astype(jnp.bfloat16)
        values = split_ref[:, lanes]
        masked = jnp.concatenate(
            [jnp.where(group_of == group, values, 0.0).astype(jnp.bfloat16) for group in range(groups)], axis=0
        )
        return total + lax.dot_general(
            masked, placed, (((1,), (1,)), ((), ())), preferred_element_type=jnp.float32
        )

    moved = lax.fori_loop(
        0, atoms // chunk, chunk_step, jnp.zeros((groups * 2 * vecs, BLK), jnp.float32)
    )
    kinds = type_ref[...]
    hardness = jnp.zeros((1, atoms), jnp.float32)
    for kind in range(hard_ref.shape[0]):
        hardness = jnp.where(kinds == kind, hard_ref[kind], hardness)
    for group in range(groups):
        lanes = slice(group * BLK, (group + 1) * BLK)
        first = group * 2 * vecs
        placed = moved[first : first + vecs] + moved[first + vecs : first + 2 * vecs]
        out_ref[:, lanes] = placed + hardness[:, lanes] * krylov_ref[:, lanes]


def scattered(order, krylov, atom_type, type_hard, parts):
    vecs, atoms = krylov.shape
    vmem = pl.BlockSpec(memory_space=pltpu.VMEM)
    return pl.pallas_call(
        scatter_kernel,
        in_specs=[vmem] * 3 + [pl.BlockSpec(memory_space=pltpu.SMEM)] + [vmem] * len(parts),
        out_specs=vmem,
        out_shape=jax.ShapeDtypeStruct((vecs, atoms), jnp.float32),
        scratch_shapes=[pltpu.VMEM((2 * vecs, atoms), jnp.float32)],
        compiler_params=pltpu.CompilerParams(vmem_limit_bytes=VMEM_BYTES),
        cost_estimate=pl.CostEstimate(
            flops=4 * vecs * atoms * atoms, bytes_accessed=24 * vecs * atoms, transcendentals=0
        ),
        name="scatter_atoms",
    )(order[None, :], krylov, atom_type[None, :], type_hard, *parts)


def lanes_of(block):
    return pl.ds(pl.multiple_of(block * BLK, BLK), BLK)


def pair_kernel(slabs, left_blocks, left_ids, right_ids, count_ref, table_ref, *refs):
    geo_refs, vec_refs = refs[:slabs], refs[slabs : 2 * slabs]
    out_refs = refs[2 * slabs : 3 * slabs]
    left_ref, origin_ref, geo_ref, mix_ref, vec_ref, acc_ref, both_ref, tile_ref = refs[3 * slabs :]
    atoms = geo_refs[0].shape[1]
    blocks = slabs * atoms // BLK
    row_id = lax.broadcasted_iota(jnp.int32, (8, BLK), 0)
    type_width = table_ref[...]

    for slab in range(slabs):
        geo_ref[:, slab * atoms : (slab + 1) * atoms] = geo_refs[slab][...]
        vec_ref[:, slab * atoms : (slab + 1) * atoms] = vec_refs[slab][...]
    acc_ref[...] = jnp.zeros_like(acc_ref)

    def one_hot(geometry):
        return jnp.where(row_id.astype(jnp.float32) == geometry[3:4, :], 1.0, 0.0)

    def mix_step(block, carry):
        hot = one_hot(geo_ref[:, lanes_of(block)])
        width = jnp.sum(hot * type_width, axis=0, keepdims=True)
        high, mid, low = split3(SLOPE * lax.rsqrt(type_width * type_width + width * width))
        mix_ref[:, lanes_of(block)] = jnp.concatenate([high, mid, low, jnp.zeros_like(low)], axis=0).astype(
            jnp.bfloat16
        )
        return carry

    lax.fori_loop(0, blocks, mix_step, 0, unroll=4)

    def left_step(block, carry):
        geometry = geo_ref[:, lanes_of(block)]
        hot = one_hot(geometry)
        origin = jnp.broadcast_to(geometry[:, 0:1], (8, BLK))
        origin_ref[block] = origin
        local = jnp.where(row_id < 3, geometry - origin, 0.0)
        norm = jnp.sum(local * local, axis=0, keepdims=True) + SOFTENING * SOFTENING
        side = jnp.where(row_id < 3, -2.0 * local, jnp.where(row_id == 3, 1.0, jnp.where(row_id == 4, norm, 0.0)))
        high, mid, low = split3(side)
        rows = jnp.concatenate(
            [high, high, mid, mid, high, low, hot, hot, hot, jnp.zeros((BLK - 72, BLK), jnp.float32)], axis=0
        )
        left_ref[block] = rows.T.astype(jnp.bfloat16)
        return carry

    lax.fori_loop(0, left_blocks, left_step, 0, unroll=4)

    both_ref[...] = jnp.ones_like(both_ref)
    tile_ref[...] = jnp.zeros_like(tile_ref)
    slots = left_ids.shape[0]
    live = count_ref[0]
    zero_side = jnp.zeros((48, BLK), jnp.bfloat16)
    zero_mix = jnp.zeros((32, BLK), jnp.bfloat16)
    zero_tail = jnp.zeros((BLK - 80, 2 * BLK), jnp.bfloat16)

    def weights_of(left, right):
        geometry = geo_ref[:, lanes_of(right)]
        local = jnp.where(row_id < 3, geometry - origin_ref[left], 0.0)
        norm = jnp.sum(local * local, axis=0, keepdims=True)
        side = jnp.where(row_id == 3, norm, jnp.where(row_id == 4, 1.0, local))
        high, mid, low = split3(side)
        rows = jnp.concatenate([high, mid, high, mid, low, high], axis=0).astype(jnp.bfloat16)
        mix = mix_ref[:, lanes_of(right)]
        return jnp.concatenate(
            [
                jnp.concatenate([rows, zero_side], axis=1),
                jnp.concatenate([zero_mix, mix], axis=1),
                zero_tail,
            ],
            axis=0,
        )

    def screened(square, inverse_width):
        inverse = lax.rsqrt(square)
        scaled = square * inverse * inverse_width
        narrow = scaled.astype(jnp.bfloat16)
        power = narrow * narrow
        series = jnp.bfloat16(ERF_SERIES[-1])
        for factor in ERF_SERIES[-2::-1] + (1.0,):
            series = series * power + jnp.bfloat16(factor)
        return (jnp.tanh(narrow * series).astype(jnp.float32) * inverse).astype(jnp.bfloat16)

    def slot_ids(turn, offset):
        slot = turn * UNROLL + offset
        place = jnp.clip(slot, 0, slots - 1)
        return left_ids[place], right_ids[place], (slot >= 0) & (slot < live)

    def pair_step(turn, carry):
        done = []
        for offset in range(UNROLL):
            left, right, alive = slot_ids(turn - 2, offset)
            tile = tile_ref[offset]
            forward = lax.dot_general(
                vec_ref[:, lanes_of(right)], tile, (((1,), (1,)), ((), ())), preferred_element_type=jnp.float32
            )
            backward = jnp.dot(vec_ref[:, lanes_of(left)], tile, preferred_element_type=jnp.float32)
            done.append((left, right, forward, backward, alive))
        for offset in range(UNROLL):
            for first in range(0, BLK, CHUNK):
                rows = slice(first, first + CHUNK)
                tile_ref[offset, rows] = screened(both_ref[offset, rows, :BLK], both_ref[offset, rows, BLK:])
        for offset in range(UNROLL):
            left, right, _ = slot_ids(turn, offset)
            both_ref[offset] = jnp.dot(
                left_ref[left], weights_of(left, right), preferred_element_type=jnp.float32
            )
        for left, right, forward, backward, alive in done:
            acc_ref[:, lanes_of(left)] += jnp.where(alive, forward, 0.0)
            acc_ref[:, lanes_of(right)] += jnp.where(alive & (left != right), backward, 0.0)
        return carry

    lax.fori_loop(0, (live + UNROLL - 1) // UNROLL + 2, pair_step, 0)

    for slab in range(slabs):
        out_refs[slab][...] = acc_ref[:, slab * atoms : (slab + 1) * atoms].astype(out_refs[slab].dtype)


def pair_sums(geometries, vectors, left_ids, right_ids, count, table, left_blocks):
    slabs = len(geometries)
    atoms = geometries[0].shape[1]
    vecs = vectors[0].shape[0]
    smem = pl.BlockSpec(memory_space=pltpu.SMEM)
    vmem = pl.BlockSpec(memory_space=pltpu.VMEM)
    kinds = [jnp.float32] + [jnp.bfloat16] * (slabs - 1)
    return pl.pallas_call(
        functools.partial(pair_kernel, slabs, left_blocks),
        in_specs=[smem] * 3 + [vmem] * (1 + 2 * slabs),
        out_specs=[vmem] * slabs,
        out_shape=[jax.ShapeDtypeStruct((vecs, atoms), kind) for kind in kinds],
        scratch_shapes=[
            pltpu.VMEM((left_blocks, BLK, BLK), jnp.bfloat16),
            pltpu.VMEM((left_blocks, 8, BLK), jnp.float32),
            pltpu.VMEM((8, slabs * atoms), jnp.float32),
            pltpu.VMEM((32, slabs * atoms), jnp.bfloat16),
            pltpu.VMEM((vecs, slabs * atoms), jnp.bfloat16),
            pltpu.VMEM((vecs, slabs * atoms), jnp.float32),
            pltpu.VMEM((UNROLL, BLK, 2 * BLK), jnp.float32),
            pltpu.VMEM((UNROLL, BLK, BLK), jnp.bfloat16),
        ],
        compiler_params=pltpu.CompilerParams(vmem_limit_bytes=VMEM_BYTES),
        cost_estimate=pl.CostEstimate(
            flops=left_ids.shape[0] * BLK * BLK * (4 * vecs + 320),
            bytes_accessed=slabs * atoms * (32 + 4 * vecs),
            transcendentals=2 * left_ids.shape[0] * BLK * BLK,
        ),
        name="pair_sums",
    )(left_ids, right_ids, count, table, *geometries, *vectors)


def along_row(value, steps):
    count = lax.axis_size("row")
    first, last = max(0, -steps), min(count, count - steps)
    return lax.ppermute(value, "row", [(source, source + steps) for source in range(first, last)])


def along_col(value, steps):
    count = lax.axis_size("col")
    return lax.ppermute(value, "col", [(source, (source + steps) % count) for source in range(count)])


def on_device(
    positions, atom_type, krylov, block_order, type_width, type_hard, pair_rows, pair_cols, pair_count
):
    vecs, atoms = krylov.shape
    shard_blocks = atoms // BLK
    geometry, vectors = gathered(positions, atom_type, krylov, block_order)

    col_devices = lax.axis_size("col")
    peers = [("col", step) for step in range(1, col_devices)] + [("row", 1), ("row", 2)]
    moved = {"col": along_col, "row": along_row}
    geometries = [geometry] + [moved[axis](geometry, -step) for axis, step in peers]
    panels = [vectors] + [moved[axis](vectors, -step) for axis, step in peers]

    row_index = lax.axis_index("row")
    col_index = lax.axis_index("col")
    rows_list = pair_rows.reshape(-1)
    cols_list = pair_cols.reshape(-1)
    row_slab = (rows_list // shard_blocks - col_index + col_devices) % col_devices
    left_ids = row_slab * shard_blocks + rows_list % shard_blocks
    step = jnp.clip(cols_list // shard_blocks - row_index, 0, 2)
    right_slab = jnp.where(step == 0, 0, step + col_devices - 1)
    right_ids = right_slab * shard_blocks + cols_list % shard_blocks
    table = jnp.zeros((8, BLK), jnp.float32) + jnp.pad(
        type_width, (0, 8 - type_width.shape[0]), constant_values=1.0
    )[:, None]
    sums = pair_sums(
        geometries, panels, left_ids, right_ids, pair_count.reshape(1), table, col_devices * shard_blocks
    )
    returned = [sums[0]] + [moved[axis](part, step) for (axis, step), part in zip(peers, sums[1:])]
    return scattered(block_order, krylov, atom_type, type_hard, returned)


def solution(mesh):
    placed = (
        P(None, ("row", "col")),
        P(("row", "col")),
        P(None, ("row", "col")),
        P(("row", "col")),
        P(),
        P(),
        P("row", "col", None),
        P("row", "col", None),
        P("row", "col"),
    )
    return jax.shard_map(
        on_device, mesh=mesh, in_specs=placed, out_specs=P(None, ("row", "col")), check_vma=False
    )
```

```python
import functools

import jax
import jax.numpy as jnp
from jax import lax
from jax.experimental import pallas as pl
from jax.experimental.pallas import tpu as pltpu
from jax.sharding import PartitionSpec as P

BLK = 128
SOFTENING = 0.5
UNROLL = 8
CHUNK = 32
VMEM_BYTES = 56 * 1024 * 1024
SLOPE = 1.1283737853323306
ERF_SERIES = (
    0.07159415430567773,
    -0.00022649025157034893,
    -0.000190667906232071,
    1.1875337467865749e-05,
)


def split3(values):
    high = values.astype(jnp.bfloat16).astype(jnp.float32)
    rest = values - high
    mid = rest.astype(jnp.bfloat16).astype(jnp.float32)
    low = (rest - mid).astype(jnp.bfloat16).astype(jnp.float32)
    return high, mid, low


def gather_kernel(place_ref, type_ref, krylov_ref, order_ref, geometry_ref, vectors_ref, stacked_ref):
    atoms = place_ref.shape[1]
    vecs = krylov_ref.shape[0]
    groups = atoms // BLK
    rows = 16 + vecs
    width = order_ref.shape[1]

    @pl.when(pl.program_id(0) == 0)
    def _():
        high, mid, low = split3(place_ref[...])
        kinds = type_ref[...].astype(jnp.float32)
        empty = jnp.zeros((6, atoms), jnp.float32)
        full = jnp.concatenate([high, mid, low, kinds, empty, krylov_ref[...]], axis=0).astype(jnp.bfloat16)
        for group in range(groups):
            stacked_ref[group * rows : (group + 1) * rows] = full[:, group * BLK : (group + 1) * BLK]

    order = order_ref[...]
    group_of, lane_of = order // BLK, order % BLK
    lane_ids = lax.broadcasted_iota(jnp.int32, (BLK, width), 0)
    picked = (lane_ids == lane_of).astype(jnp.float32).astype(jnp.bfloat16)
    total = jnp.zeros((rows, width), jnp.float32)
    for group in range(groups):
        here = jnp.dot(
            stacked_ref[group * rows : (group + 1) * rows], picked, preferred_element_type=jnp.float32
        )
        total = jnp.where(group_of == group, here, total)
    place = total[0:3] + total[3:6] + total[6:9]
    geometry_ref[...] = jnp.concatenate([place, total[9:10], jnp.zeros((4, width), jnp.float32)], axis=0)
    vectors_ref[...] = total[16:].astype(jnp.bfloat16)


def gathered(positions, atom_type, krylov, order, tile=512):
    vecs, atoms = krylov.shape
    return pl.pallas_call(
        gather_kernel,
        grid=(atoms // tile,),
        in_specs=[
            pl.BlockSpec((3, atoms), lambda step: (0, 0)),
            pl.BlockSpec((1, atoms), lambda step: (0, 0)),
            pl.BlockSpec((vecs, atoms), lambda step: (0, 0)),
            pl.BlockSpec((1, tile), lambda step: (0, step)),
        ],
        out_specs=[
            pl.BlockSpec((8, tile), lambda step: (0, step)),
            pl.BlockSpec((vecs, tile), lambda step: (0, step)),
        ],
        out_shape=[
            jax.ShapeDtypeStruct((8, atoms), jnp.float32),
            jax.ShapeDtypeStruct((vecs, atoms), jnp.bfloat16),
        ],
        scratch_shapes=[pltpu.VMEM((atoms // BLK * (16 + vecs), BLK), jnp.bfloat16)],
        compiler_params=pltpu.CompilerParams(vmem_limit_bytes=VMEM_BYTES),
        cost_estimate=pl.CostEstimate(
            flops=2 * (16 + vecs) * atoms * atoms, bytes_accessed=8 * vecs * atoms, transcendentals=0
        ),
        name="gather_atoms",
    )(positions, atom_type[None, :], krylov, order[None, :])


def scatter_kernel(order_ref, krylov_ref, type_ref, hard_ref, valid_ref, *refs):
    parts, (out_ref, split_ref) = refs[:-2], refs[-2:]
    vecs, atoms = krylov_ref.shape
    groups = atoms // BLK
    chunk = 512
    total = parts[0][...]
    for index, part in enumerate(parts[1:]):
        total = total + jnp.where(valid_ref[index] > 0, part[...].astype(jnp.float32), 0.0)
    high = total.astype(jnp.bfloat16).astype(jnp.float32)
    split_ref[0:vecs] = high
    split_ref[vecs:] = total - high

    lane_ids = lax.broadcasted_iota(jnp.int32, (BLK, chunk), 0)

    def chunk_step(step, total):
        lanes = pl.ds(pl.multiple_of(step * chunk, chunk), chunk)
        order = order_ref[:, lanes]
        group_of, lane_of = order // BLK, order % BLK
        placed = (lane_ids == lane_of).astype(jnp.float32).astype(jnp.bfloat16)
        values = split_ref[:, lanes]
        masked = jnp.concatenate(
            [jnp.where(group_of == group, values, 0.0).astype(jnp.bfloat16) for group in range(groups)], axis=0
        )
        return total + lax.dot_general(
            masked, placed, (((1,), (1,)), ((), ())), preferred_element_type=jnp.float32
        )

    moved = lax.fori_loop(
        0, atoms // chunk, chunk_step, jnp.zeros((groups * 2 * vecs, BLK), jnp.float32)
    )
    kinds = type_ref[...]
    hardness = jnp.zeros((1, atoms), jnp.float32)
    for kind in range(hard_ref.shape[0]):
        hardness = jnp.where(kinds == kind, hard_ref[kind], hardness)
    for group in range(groups):
        lanes = slice(group * BLK, (group + 1) * BLK)
        first = group * 2 * vecs
        placed = moved[first : first + vecs] + moved[first + vecs : first + 2 * vecs]
        out_ref[:, lanes] = placed + hardness[:, lanes] * krylov_ref[:, lanes]


def scattered(order, krylov, atom_type, type_hard, valid, parts):
    vecs, atoms = krylov.shape
    vmem = pl.BlockSpec(memory_space=pltpu.VMEM)
    return pl.pallas_call(
        scatter_kernel,
        in_specs=[vmem] * 3 + [pl.BlockSpec(memory_space=pltpu.SMEM)] * 2 + [vmem] * len(parts),
        out_specs=vmem,
        out_shape=jax.ShapeDtypeStruct((vecs, atoms), jnp.float32),
        scratch_shapes=[pltpu.VMEM((2 * vecs, atoms), jnp.float32)],
        compiler_params=pltpu.CompilerParams(vmem_limit_bytes=VMEM_BYTES),
        cost_estimate=pl.CostEstimate(
            flops=4 * vecs * atoms * atoms, bytes_accessed=24 * vecs * atoms, transcendentals=0
        ),
        name="scatter_atoms",
    )(order[None, :], krylov, atom_type[None, :], type_hard, valid, *parts)


def lanes_of(block):
    return pl.ds(pl.multiple_of(block * BLK, BLK), BLK)


def pair_kernel(slabs, left_blocks, left_ids, right_ids, count_ref, table_ref, *refs):
    geo_refs, vec_refs = refs[:slabs], refs[slabs : 2 * slabs]
    out_refs = refs[2 * slabs : 3 * slabs]
    left_ref, origin_ref, geo_ref, mix_ref, vec_ref, acc_ref, both_ref, tile_ref = refs[3 * slabs :]
    atoms = geo_refs[0].shape[1]
    blocks = slabs * atoms // BLK
    row_id = lax.broadcasted_iota(jnp.int32, (8, BLK), 0)
    type_width = table_ref[...]

    for slab in range(slabs):
        geo_ref[:, slab * atoms : (slab + 1) * atoms] = geo_refs[slab][...]
        vec_ref[:, slab * atoms : (slab + 1) * atoms] = vec_refs[slab][...]
    acc_ref[...] = jnp.zeros_like(acc_ref)

    def one_hot(geometry):
        return jnp.where(row_id.astype(jnp.float32) == geometry[3:4, :], 1.0, 0.0)

    def mix_step(block, carry):
        hot = one_hot(geo_ref[:, lanes_of(block)])
        width = jnp.sum(hot * type_width, axis=0, keepdims=True)
        high, mid, low = split3(SLOPE * lax.rsqrt(type_width * type_width + width * width))
        mix_ref[:, lanes_of(block)] = jnp.concatenate([high, mid, low, jnp.zeros_like(low)], axis=0).astype(
            jnp.bfloat16
        )
        return carry

    lax.fori_loop(0, blocks, mix_step, 0, unroll=4)

    def left_step(block, carry):
        geometry = geo_ref[:, lanes_of(block)]
        hot = one_hot(geometry)
        origin = jnp.broadcast_to(geometry[:, 0:1], (8, BLK))
        origin_ref[block] = origin
        local = jnp.where(row_id < 3, geometry - origin, 0.0)
        norm = jnp.sum(local * local, axis=0, keepdims=True) + SOFTENING * SOFTENING
        side = jnp.where(row_id < 3, -2.0 * local, jnp.where(row_id == 3, 1.0, jnp.where(row_id == 4, norm, 0.0)))
        high, mid, low = split3(side)
        rows = jnp.concatenate(
            [high, high, mid, mid, high, low, hot, hot, hot, jnp.zeros((BLK - 72, BLK), jnp.float32)], axis=0
        )
        left_ref[block] = rows.T.astype(jnp.bfloat16)
        return carry

    lax.fori_loop(0, left_blocks, left_step, 0, unroll=4)

    both_ref[...] = jnp.ones_like(both_ref)
    tile_ref[...] = jnp.zeros_like(tile_ref)
    slots = left_ids.shape[0]
    live = count_ref[0]
    zero_side = jnp.zeros((48, BLK), jnp.bfloat16)
    zero_mix = jnp.zeros((32, BLK), jnp.bfloat16)
    zero_tail = jnp.zeros((BLK - 80, 2 * BLK), jnp.bfloat16)

    def weights_of(left, right):
        geometry = geo_ref[:, lanes_of(right)]
        local = jnp.where(row_id < 3, geometry - origin_ref[left], 0.0)
        norm = jnp.sum(local * local, axis=0, keepdims=True)
        side = jnp.where(row_id == 3, norm, jnp.where(row_id == 4, 1.0, local))
        high, mid, low = split3(side)
        rows = jnp.concatenate([high, mid, high, mid, low, high], axis=0).astype(jnp.bfloat16)
        mix = mix_ref[:, lanes_of(right)]
        return jnp.concatenate(
            [
                jnp.concatenate([rows, zero_side], axis=1),
                jnp.concatenate([zero_mix, mix], axis=1),
                zero_tail,
            ],
            axis=0,
        )

    def screened(square, inverse_width):
        inverse = lax.rsqrt(square)
        scaled = square * inverse * inverse_width
        narrow = scaled.astype(jnp.bfloat16)
        power = narrow * narrow
        series = jnp.bfloat16(ERF_SERIES[-1])
        for factor in ERF_SERIES[-2::-1] + (1.0,):
            series = series * power + jnp.bfloat16(factor)
        return (jnp.tanh(narrow * series).astype(jnp.float32) * inverse).astype(jnp.bfloat16)

    def slot_ids(turn, offset):
        slot = turn * UNROLL + offset
        place = jnp.clip(slot, 0, slots - 1)
        return left_ids[place], right_ids[place], (slot >= 0) & (slot < live)

    def pair_step(turn, carry):
        done = []
        for offset in range(UNROLL):
            left, right, alive = slot_ids(turn - 2, offset)
            tile = tile_ref[offset]
            forward = lax.dot_general(
                vec_ref[:, lanes_of(right)], tile, (((1,), (1,)), ((), ())), preferred_element_type=jnp.float32
            )
            backward = jnp.dot(vec_ref[:, lanes_of(left)], tile, preferred_element_type=jnp.float32)
            done.append((left, right, forward, backward, alive))
        for offset in range(UNROLL):
            for first in range(0, BLK, CHUNK):
                rows = slice(first, first + CHUNK)
                tile_ref[offset, rows] = screened(both_ref[offset, rows, :BLK], both_ref[offset, rows, BLK:])
        for offset in range(UNROLL):
            left, right, _ = slot_ids(turn, offset)
            both_ref[offset] = jnp.dot(
                left_ref[left], weights_of(left, right), preferred_element_type=jnp.float32
            )
        for left, right, forward, backward, alive in done:
            acc_ref[:, lanes_of(left)] += jnp.where(alive, forward, 0.0)
            acc_ref[:, lanes_of(right)] += jnp.where(alive & (left != right), backward, 0.0)
        return carry

    lax.fori_loop(0, (live + UNROLL - 1) // UNROLL + 2, pair_step, 0)

    for slab in range(slabs):
        out_refs[slab][...] = acc_ref[:, slab * atoms : (slab + 1) * atoms].astype(out_refs[slab].dtype)


def pair_sums(geometries, vectors, left_ids, right_ids, count, table, left_blocks):
    slabs = len(geometries)
    atoms = geometries[0].shape[1]
    vecs = vectors[0].shape[0]
    smem = pl.BlockSpec(memory_space=pltpu.SMEM)
    vmem = pl.BlockSpec(memory_space=pltpu.VMEM)
    kinds = [jnp.float32] + [jnp.bfloat16] * (slabs - 1)
    return pl.pallas_call(
        functools.partial(pair_kernel, slabs, left_blocks),
        in_specs=[smem] * 3 + [vmem] * (1 + 2 * slabs),
        out_specs=[vmem] * slabs,
        out_shape=[jax.ShapeDtypeStruct((vecs, atoms), kind) for kind in kinds],
        scratch_shapes=[
            pltpu.VMEM((left_blocks, BLK, BLK), jnp.bfloat16),
            pltpu.VMEM((left_blocks, 8, BLK), jnp.float32),
            pltpu.VMEM((8, slabs * atoms), jnp.float32),
            pltpu.VMEM((32, slabs * atoms), jnp.bfloat16),
            pltpu.VMEM((vecs, slabs * atoms), jnp.bfloat16),
            pltpu.VMEM((vecs, slabs * atoms), jnp.float32),
            pltpu.VMEM((UNROLL, BLK, 2 * BLK), jnp.float32),
            pltpu.VMEM((UNROLL, BLK, BLK), jnp.bfloat16),
        ],
        compiler_params=pltpu.CompilerParams(vmem_limit_bytes=VMEM_BYTES),
        cost_estimate=pl.CostEstimate(
            flops=left_ids.shape[0] * BLK * BLK * (4 * vecs + 320),
            bytes_accessed=slabs * atoms * (32 + 4 * vecs),
            transcendentals=2 * left_ids.shape[0] * BLK * BLK,
        ),
        name="pair_sums",
    )(left_ids, right_ids, count, table, *geometries, *vectors)


def exchange_kernel(peers, toward, items, *refs):
    count = len(peers) * items
    sources, targets = refs[:count], refs[count : 2 * count]
    send_sems, recv_sems = refs[2 * count :]
    barrier = pltpu.get_barrier_semaphore()

    def neighbour(axis, shift):
        size, here = lax.axis_size(axis), lax.axis_index(axis)
        there = here + shift
        if axis == "col":
            return {axis: lax.rem(there + size, size)}, there == there
        return {axis: there}, (there >= 0) & (there < size)

    expected = jnp.int32(0)
    for axis, step in peers:
        device, exists = neighbour(axis, -toward * step)

        @pl.when(exists)
        def _():
            pl.semaphore_signal(barrier, inc=1, device_id=device, device_id_type=pl.DeviceIdType.MESH)

        expected = expected + neighbour(axis, toward * step)[1].astype(jnp.int32)
    pl.semaphore_wait(barrier, expected)

    def copy_of(index):
        axis, step = peers[index // items]
        device, exists = neighbour(axis, toward * step)
        copy = pltpu.make_async_remote_copy(
            src_ref=sources[index],
            dst_ref=targets[index],
            send_sem=send_sems.at[index],
            recv_sem=recv_sems.at[index],
            device_id=device,
            device_id_type=pl.DeviceIdType.MESH,
        )
        return copy, exists, neighbour(axis, -toward * step)[1]

    for index in range(count):
        copy, exists, _ = copy_of(index)
        pl.when(exists)(copy.start)
    for index in range(count):
        copy, exists, arrives = copy_of(index)
        pl.when(exists)(copy.wait_send)
        pl.when(arrives)(copy.wait_recv)


def exchanged(panels, peers, toward, collective_id):
    items = len(panels[0])
    flat = [item for panel in panels for item in panel]
    moved = pl.pallas_call(
        functools.partial(exchange_kernel, peers, toward, items),
        in_specs=[pl.BlockSpec(memory_space=pl.ANY)] * len(flat),
        out_specs=[pl.BlockSpec(memory_space=pl.ANY)] * len(flat),
        out_shape=[jax.ShapeDtypeStruct(item.shape, item.dtype) for item in flat],
        scratch_shapes=[pltpu.SemaphoreType.DMA((len(flat),)), pltpu.SemaphoreType.DMA((len(flat),))],
        compiler_params=pltpu.CompilerParams(
            collective_id=collective_id, has_side_effects=True, vmem_limit_bytes=VMEM_BYTES
        ),
        name="send_atoms" if collective_id == 0 else "return_sums",
    )(*flat)
    return [moved[first : first + items] for first in range(0, len(flat), items)]


def on_device(
    positions, atom_type, krylov, block_order, type_width, type_hard, pair_rows, pair_cols, pair_count
):
    vecs, atoms = krylov.shape
    shard_blocks = atoms // BLK
    geometry, vectors = gathered(positions, atom_type, krylov, block_order)

    col_devices = lax.axis_size("col")
    peers = [("col", step) for step in range(1, col_devices)] + [("row", 1), ("row", 2)]
    arrived = exchanged([(geometry, vectors)] * len(peers), peers, -1, 0)
    geometries = [geometry] + [panel[0] for panel in arrived]
    panels = [vectors] + [panel[1] for panel in arrived]

    row_index = lax.axis_index("row")
    col_index = lax.axis_index("col")
    rows_list = pair_rows.reshape(-1)
    cols_list = pair_cols.reshape(-1)
    row_slab = (rows_list // shard_blocks - col_index + col_devices) % col_devices
    left_ids = row_slab * shard_blocks + rows_list % shard_blocks
    step = jnp.clip(cols_list // shard_blocks - row_index, 0, 2)
    right_slab = jnp.where(step == 0, 0, step + col_devices - 1)
    right_ids = right_slab * shard_blocks + cols_list % shard_blocks
    table = jnp.zeros((8, BLK), jnp.float32) + jnp.pad(
        type_width, (0, 8 - type_width.shape[0]), constant_values=1.0
    )[:, None]
    sums = pair_sums(
        geometries, panels, left_ids, right_ids, pair_count.reshape(1), table, col_devices * shard_blocks
    )
    returned = [panel[0] for panel in exchanged([(part,) for part in sums[1:]], peers, 1, 1)]
    valid = jnp.stack([jnp.int32(1) if axis == "col" else (row_index >= step).astype(jnp.int32) for axis, step in peers])
    return scattered(block_order, krylov, atom_type, type_hard, valid, [sums[0]] + returned)


def solution(mesh):
    placed = (
        P(None, ("row", "col")),
        P(("row", "col")),
        P(None, ("row", "col")),
        P(("row", "col")),
        P(),
        P(),
        P("row", "col", None),
        P("row", "col", None),
        P("row", "col"),
    )
    return jax.shard_map(
        on_device, mesh=mesh, in_specs=placed, out_specs=P(None, ("row", "col")), check_vma=False
    )
```

```python
import functools

import jax
import jax.numpy as jnp
from jax import lax
from jax.experimental import pallas as pl
from jax.experimental.pallas import tpu as pltpu
from jax.sharding import PartitionSpec as P

BLK = 128
SOFTENING = 0.5
UNROLL = 16
CHUNK = 32
VMEM_BYTES = 56 * 1024 * 1024
SLOPE = 1.1283737853323306
ERF_SERIES = (
    0.07159415430567773,
    -0.00022649025157034893,
    -0.000190667906232071,
    1.1875337467865749e-05,
)


def split3(values):
    high = values.astype(jnp.bfloat16).astype(jnp.float32)
    rest = values - high
    mid = rest.astype(jnp.bfloat16).astype(jnp.float32)
    low = (rest - mid).astype(jnp.bfloat16).astype(jnp.float32)
    return high, mid, low


def gather_kernel(place_ref, type_ref, krylov_ref, order_ref, geometry_ref, vectors_ref, stacked_ref):
    atoms = place_ref.shape[1]
    vecs = krylov_ref.shape[0]
    groups = atoms // BLK
    rows = 16 + vecs
    width = 2 * BLK
    together = 8
    high, mid, low = split3(place_ref[...])
    kinds = type_ref[...].astype(jnp.float32)
    empty = jnp.zeros((6, atoms), jnp.float32)
    full = jnp.concatenate([high, mid, low, kinds, empty, krylov_ref[...]], axis=0).astype(jnp.bfloat16)
    for group in range(groups):
        stacked_ref[group * rows : (group + 1) * rows] = full[:, group * BLK : (group + 1) * BLK]
    lane_ids = lax.broadcasted_iota(jnp.int32, (BLK, width), 0)

    def chunk_step(step, carry):
        lanes = pl.ds(pl.multiple_of(step * width, width), width)
        order = order_ref[:, lanes]
        picked = (lane_ids == order % BLK).astype(jnp.float32).astype(jnp.bfloat16)
        group_of = jnp.broadcast_to(order // BLK, (rows, width))
        total = jnp.zeros((rows, width), jnp.float32)
        for first in range(0, groups, together):
            here = jnp.dot(
                stacked_ref[first * rows : (first + together) * rows], picked, preferred_element_type=jnp.float32
            )
            for offset in range(together):
                part = here[offset * rows : (offset + 1) * rows]
                total = jnp.where(group_of == first + offset, part, total)
        place = total[0:3] + total[3:6] + total[6:9]
        geometry_ref[:, lanes] = jnp.concatenate([place, total[9:10]], axis=0)
        vectors_ref[:, lanes] = total[16:].astype(jnp.bfloat16)
        return carry

    lax.fori_loop(0, atoms // width, chunk_step, 0, unroll=2)


def gathered(positions, atom_type, krylov, order):
    vecs, atoms = krylov.shape
    vmem = pl.BlockSpec(memory_space=pltpu.VMEM)
    return pl.pallas_call(
        gather_kernel,
        in_specs=[vmem] * 4,
        out_specs=[vmem] * 2,
        out_shape=[
            jax.ShapeDtypeStruct((4, atoms), jnp.float32),
            jax.ShapeDtypeStruct((vecs, atoms), jnp.bfloat16),
        ],
        scratch_shapes=[pltpu.VMEM((atoms // BLK * (16 + vecs), BLK), jnp.bfloat16)],
        compiler_params=pltpu.CompilerParams(vmem_limit_bytes=VMEM_BYTES),
        cost_estimate=pl.CostEstimate(
            flops=2 * (16 + vecs) * atoms * atoms, bytes_accessed=8 * vecs * atoms, transcendentals=0
        ),
        name="gather_atoms",
    )(positions, atom_type[None, :], krylov, order[None, :])


def scatter_kernel(order_ref, krylov_ref, type_ref, hard_ref, valid_ref, *refs):
    parts, (out_ref, split_ref) = refs[:-2], refs[-2:]
    vecs, atoms = krylov_ref.shape
    groups = atoms // BLK
    chunk = 1024
    total = parts[0][...]
    for index, part in enumerate(parts[1:]):
        total = total + jnp.where(valid_ref[index] > 0, part[...].astype(jnp.float32), 0.0)
    high = total.astype(jnp.bfloat16).astype(jnp.float32)
    split_ref[0:vecs] = high
    split_ref[vecs:] = total - high

    lane_ids = lax.broadcasted_iota(jnp.int32, (BLK, chunk), 0)

    def chunk_step(step, total):
        lanes = pl.ds(pl.multiple_of(step * chunk, chunk), chunk)
        order = order_ref[:, lanes]
        group_of, lane_of = order // BLK, order % BLK
        placed = (lane_ids == lane_of).astype(jnp.float32).astype(jnp.bfloat16)
        values = split_ref[:, lanes]
        masked = jnp.concatenate(
            [jnp.where(group_of == group, values, 0.0).astype(jnp.bfloat16) for group in range(groups)], axis=0
        )
        return total + lax.dot_general(
            masked, placed, (((1,), (1,)), ((), ())), preferred_element_type=jnp.float32
        )

    moved = lax.fori_loop(
        0, atoms // chunk, chunk_step, jnp.zeros((groups * 2 * vecs, BLK), jnp.float32)
    )
    kinds = type_ref[...]
    hardness = jnp.zeros((1, atoms), jnp.float32)
    for kind in range(hard_ref.shape[0]):
        hardness = jnp.where(kinds == kind, hard_ref[kind], hardness)
    for group in range(groups):
        lanes = slice(group * BLK, (group + 1) * BLK)
        first = group * 2 * vecs
        placed = moved[first : first + vecs] + moved[first + vecs : first + 2 * vecs]
        out_ref[:, lanes] = placed + hardness[:, lanes] * krylov_ref[:, lanes]


def scattered(order, krylov, atom_type, type_hard, valid, parts):
    vecs, atoms = krylov.shape
    vmem = pl.BlockSpec(memory_space=pltpu.VMEM)
    return pl.pallas_call(
        scatter_kernel,
        in_specs=[vmem] * 3 + [pl.BlockSpec(memory_space=pltpu.SMEM)] * 2 + [vmem] * len(parts),
        out_specs=vmem,
        out_shape=jax.ShapeDtypeStruct((vecs, atoms), jnp.float32),
        scratch_shapes=[pltpu.VMEM((2 * vecs, atoms), jnp.float32)],
        compiler_params=pltpu.CompilerParams(vmem_limit_bytes=VMEM_BYTES),
        cost_estimate=pl.CostEstimate(
            flops=4 * vecs * atoms * atoms, bytes_accessed=24 * vecs * atoms, transcendentals=0
        ),
        name="scatter_atoms",
    )(order[None, :], krylov, atom_type[None, :], type_hard, valid, *parts)


def lanes_of(block):
    return pl.ds(pl.multiple_of(block * BLK, BLK), BLK)


def pair_kernel(slabs, left_blocks, left_ids, right_ids, count_ref, width_ref, *refs):
    geo_refs, vec_refs = refs[:slabs], refs[slabs : 2 * slabs]
    out_refs = refs[2 * slabs : 3 * slabs]
    left_ref, origin_ref, geo_ref, mix_ref, vec_ref, acc_ref, both_ref, tile_ref = refs[3 * slabs :]
    atoms = geo_refs[0].shape[1]
    blocks = slabs * atoms // BLK
    row_id = lax.broadcasted_iota(jnp.int32, (8, BLK), 0)
    type_width = jnp.ones((8, BLK), jnp.float32)
    for kind in range(width_ref.shape[0]):
        type_width = jnp.where(row_id == kind, width_ref[kind], type_width)
    geo_ref[4:8] = jnp.zeros((4, geo_ref.shape[1]), jnp.float32)

    for slab in range(slabs):
        geo_ref[0:4, slab * atoms : (slab + 1) * atoms] = geo_refs[slab][...]
        vec_ref[:, slab * atoms : (slab + 1) * atoms] = vec_refs[slab][...]
    acc_ref[...] = jnp.zeros_like(acc_ref)

    def one_hot(geometry):
        return jnp.where(row_id.astype(jnp.float32) == geometry[3:4, :], 1.0, 0.0)

    def mix_step(block, carry):
        hot = one_hot(geo_ref[:, lanes_of(block)])
        width = jnp.sum(hot * type_width, axis=0, keepdims=True)
        high, mid, low = split3(SLOPE * lax.rsqrt(type_width * type_width + width * width))
        mix_ref[:, lanes_of(block)] = jnp.concatenate([high, mid, low, jnp.zeros_like(low)], axis=0).astype(
            jnp.bfloat16
        )
        return carry

    lax.fori_loop(0, blocks, mix_step, 0, unroll=4)

    def left_step(block, carry):
        geometry = geo_ref[:, lanes_of(block)]
        hot = one_hot(geometry)
        origin = jnp.broadcast_to(geometry[:, 0:1], (8, BLK))
        origin_ref[block] = origin
        local = jnp.where(row_id < 3, geometry - origin, 0.0)
        norm = jnp.sum(local * local, axis=0, keepdims=True) + SOFTENING * SOFTENING
        side = jnp.where(row_id < 3, -2.0 * local, jnp.where(row_id == 3, 1.0, jnp.where(row_id == 4, norm, 0.0)))
        high, mid, low = split3(side)
        rows = jnp.concatenate(
            [high, high, mid, mid, high, low, hot, hot, hot, jnp.zeros((BLK - 72, BLK), jnp.float32)], axis=0
        )
        left_ref[block] = rows.T.astype(jnp.bfloat16)
        return carry

    lax.fori_loop(0, left_blocks, left_step, 0, unroll=4)

    both_ref[...] = jnp.ones_like(both_ref)
    tile_ref[...] = jnp.zeros_like(tile_ref)
    slots = left_ids.shape[1]
    live = count_ref[0]
    zero_side = jnp.zeros((48, BLK), jnp.bfloat16)
    zero_mix = jnp.zeros((32, BLK), jnp.bfloat16)
    zero_tail = jnp.zeros((BLK - 80, 2 * BLK), jnp.bfloat16)

    def weights_of(left, right):
        geometry = geo_ref[:, lanes_of(right)]
        local = jnp.where(row_id < 3, geometry - origin_ref[left], 0.0)
        norm = jnp.sum(local * local, axis=0, keepdims=True)
        side = jnp.where(row_id == 3, norm, jnp.where(row_id == 4, 1.0, local))
        high, mid, low = split3(side)
        rows = jnp.concatenate([high, mid, high, mid, low, high], axis=0).astype(jnp.bfloat16)
        mix = mix_ref[:, lanes_of(right)]
        return jnp.concatenate(
            [
                jnp.concatenate([rows, zero_side], axis=1),
                jnp.concatenate([zero_mix, mix], axis=1),
                zero_tail,
            ],
            axis=0,
        )

    def screened(square, inverse_width):
        inverse = lax.rsqrt(square)
        scaled = square * inverse * inverse_width
        narrow = scaled.astype(jnp.bfloat16)
        power = narrow * narrow
        series = jnp.bfloat16(ERF_SERIES[-1])
        for factor in ERF_SERIES[-2::-1] + (1.0,):
            series = series * power + jnp.bfloat16(factor)
        return (jnp.tanh(narrow * series).astype(jnp.float32) * inverse).astype(jnp.bfloat16)

    def slot_ids(turn, offset):
        slot = turn * UNROLL + offset
        place = jnp.clip(slot, 0, slots - 1)
        return left_ids[0, place], right_ids[0, place], (slot >= 0) & (slot < live)

    def pair_step(turn, carry):
        done = []
        for offset in range(UNROLL):
            left, right, alive = slot_ids(turn - 2, offset)
            tile = tile_ref[offset]
            forward = lax.dot_general(
                vec_ref[:, lanes_of(right)], tile, (((1,), (1,)), ((), ())), preferred_element_type=jnp.float32
            )
            backward = jnp.dot(vec_ref[:, lanes_of(left)], tile, preferred_element_type=jnp.float32)
            done.append((left, right, forward, backward, alive))
        for offset in range(UNROLL):
            for first in range(0, BLK, CHUNK):
                rows = slice(first, first + CHUNK)
                tile_ref[offset, rows] = screened(both_ref[offset, rows, :BLK], both_ref[offset, rows, BLK:])
        for offset in range(UNROLL):
            left, right, _ = slot_ids(turn, offset)
            both_ref[offset] = jnp.dot(
                left_ref[left], weights_of(left, right), preferred_element_type=jnp.float32
            )
        for left, right, forward, backward, alive in done:
            acc_ref[:, lanes_of(left)] += jnp.where(alive, forward, 0.0)
            acc_ref[:, lanes_of(right)] += jnp.where(alive & (left != right), backward, 0.0)
        return carry

    lax.fori_loop(0, (live + UNROLL - 1) // UNROLL + 2, pair_step, 0)

    for slab in range(slabs):
        out_refs[slab][...] = acc_ref[:, slab * atoms : (slab + 1) * atoms].astype(out_refs[slab].dtype)


def pair_sums(geometries, vectors, left_ids, right_ids, count, type_width, left_blocks):
    slabs = len(geometries)
    atoms = geometries[0].shape[1]
    vecs = vectors[0].shape[0]
    smem = pl.BlockSpec(memory_space=pltpu.SMEM)
    vmem = pl.BlockSpec(memory_space=pltpu.VMEM)
    kinds = [jnp.float32] + [jnp.bfloat16] * (slabs - 1)
    return pl.pallas_call(
        functools.partial(pair_kernel, slabs, left_blocks),
        in_specs=[smem] * 4 + [vmem] * (2 * slabs),
        out_specs=[vmem] * slabs,
        out_shape=[jax.ShapeDtypeStruct((vecs, atoms), kind) for kind in kinds],
        scratch_shapes=[
            pltpu.VMEM((left_blocks, BLK, BLK), jnp.bfloat16),
            pltpu.VMEM((left_blocks, 8, BLK), jnp.float32),
            pltpu.VMEM((8, slabs * atoms), jnp.float32),
            pltpu.VMEM((32, slabs * atoms), jnp.bfloat16),
            pltpu.VMEM((vecs, slabs * atoms), jnp.bfloat16),
            pltpu.VMEM((vecs, slabs * atoms), jnp.float32),
            pltpu.VMEM((UNROLL, BLK, 2 * BLK), jnp.float32),
            pltpu.VMEM((UNROLL, BLK, BLK), jnp.bfloat16),
        ],
        compiler_params=pltpu.CompilerParams(vmem_limit_bytes=VMEM_BYTES),
        cost_estimate=pl.CostEstimate(
            flops=left_ids.shape[1] * BLK * BLK * (4 * vecs + 320),
            bytes_accessed=slabs * atoms * (32 + 4 * vecs),
            transcendentals=2 * left_ids.shape[1] * BLK * BLK,
        ),
        name="pair_sums",
    )(left_ids, right_ids, count, type_width, *geometries, *vectors)


def exchange_kernel(peers, toward, items, meanwhile, *refs):
    count = len(peers) * items
    sources = refs[:count]
    targets, (send_sems, recv_sems) = refs[-2 - count : -2], refs[-2:]
    barrier = pltpu.get_barrier_semaphore()

    def neighbour(axis, shift):
        size, here = lax.axis_size(axis), lax.axis_index(axis)
        there = here + shift
        if axis == "col":
            return {axis: lax.rem(there + size, size)}, there == there
        return {axis: there}, (there >= 0) & (there < size)

    expected = jnp.int32(0)
    for axis, step in peers:
        device, exists = neighbour(axis, -toward * step)

        @pl.when(exists)
        def _():
            pl.semaphore_signal(barrier, inc=1, device_id=device, device_id_type=pl.DeviceIdType.MESH)

        expected = expected + neighbour(axis, toward * step)[1].astype(jnp.int32)
    pl.semaphore_wait(barrier, expected)

    def copy_of(index):
        axis, step = peers[index // items]
        device, exists = neighbour(axis, toward * step)
        copy = pltpu.make_async_remote_copy(
            src_ref=sources[index],
            dst_ref=targets[index],
            send_sem=send_sems.at[index],
            recv_sem=recv_sems.at[index],
            device_id=device,
            device_id_type=pl.DeviceIdType.MESH,
        )
        return copy, exists, neighbour(axis, -toward * step)[1]

    for index in range(count):
        copy, exists, _ = copy_of(index)
        pl.when(exists)(copy.start)
    if meanwhile is not None:
        meanwhile(*refs[count : -2 - count])
    for index in range(count):
        copy, exists, arrives = copy_of(index)
        pl.when(exists)(copy.wait_send)
        pl.when(arrives)(copy.wait_recv)


def slot_ids_kernel(shard_blocks, rows_ref, cols_ref, left_ref, right_ref):
    col_devices = lax.axis_size("col")
    rows, cols = rows_ref[...], cols_ref[...]
    row_slab = (rows // shard_blocks + (col_devices - lax.axis_index("col"))) % col_devices
    left_ref[...] = row_slab * shard_blocks + rows % shard_blocks
    step = jnp.clip(cols // shard_blocks - lax.axis_index("row"), 0, 2)
    right_slab = jnp.where(step == 0, 0, step + col_devices - 1)
    right_ref[...] = right_slab * shard_blocks + cols % shard_blocks


def exchanged(panels, peers, toward, collective_id, meanwhile=None, extras=(), extra_outs=()):
    items = len(panels[0])
    flat = [item for panel in panels for item in panel]
    vmem = pl.BlockSpec(memory_space=pltpu.VMEM)
    results = pl.pallas_call(
        functools.partial(exchange_kernel, peers, toward, items, meanwhile),
        in_specs=[pl.BlockSpec(memory_space=pl.ANY)] * len(flat) + [vmem] * len(extras),
        out_specs=[vmem] * len(extra_outs) + [pl.BlockSpec(memory_space=pl.ANY)] * len(flat),
        out_shape=list(extra_outs) + [jax.ShapeDtypeStruct(item.shape, item.dtype) for item in flat],
        scratch_shapes=[pltpu.SemaphoreType.DMA((len(flat),)), pltpu.SemaphoreType.DMA((len(flat),))],
        compiler_params=pltpu.CompilerParams(
            collective_id=collective_id, has_side_effects=True, vmem_limit_bytes=VMEM_BYTES
        ),
        name="send_atoms" if collective_id == 0 else "return_sums",
    )(*flat, *extras)
    moved = results[len(extra_outs) :]
    arrived = [moved[first : first + items] for first in range(0, len(flat), items)]
    return arrived, results[: len(extra_outs)]


def on_device(
    positions, atom_type, krylov, block_order, type_width, type_hard, pair_rows, pair_cols, pair_count
):
    vecs, atoms = krylov.shape
    shard_blocks = atoms // BLK
    geometry, vectors = gathered(positions, atom_type, krylov, block_order)

    col_devices = lax.axis_size("col")
    peers = [("col", step) for step in range(1, col_devices)] + [("row", 1), ("row", 2)]
    rows_list = pair_rows.reshape(1, -1)
    cols_list = pair_cols.reshape(1, -1)
    ids = jax.ShapeDtypeStruct(rows_list.shape, jnp.int32)
    arrived, (left_ids, right_ids) = exchanged(
        [(geometry, vectors)] * len(peers),
        peers,
        -1,
        0,
        functools.partial(slot_ids_kernel, shard_blocks),
        (rows_list, cols_list),
        (ids, ids),
    )
    geometries = [geometry] + [panel[0] for panel in arrived]
    panels = [vectors] + [panel[1] for panel in arrived]
    sums = pair_sums(
        geometries, panels, left_ids, right_ids, pair_count.reshape(1), type_width, col_devices * shard_blocks
    )
    returned, _ = exchanged([(part,) for part in sums[1:]], peers, 1, 1)
    row_index = lax.axis_index("row")
    valid = jnp.stack([jnp.int32(1) if axis == "col" else (row_index >= step).astype(jnp.int32) for axis, step in peers])
    return scattered(block_order, krylov, atom_type, type_hard, valid, [sums[0]] + [panel[0] for panel in returned])


def solution(mesh):
    placed = (
        P(None, ("row", "col")),
        P(("row", "col")),
        P(None, ("row", "col")),
        P(("row", "col")),
        P(),
        P(),
        P("row", "col", None),
        P("row", "col", None),
        P("row", "col"),
    )
    return jax.shard_map(
        on_device, mesh=mesh, in_specs=placed, out_specs=P(None, ("row", "col")), check_vma=False
    )
```

```python
import functools

import jax
import jax.numpy as jnp
from jax import lax
from jax.experimental import pallas as pl
from jax.experimental.pallas import tpu as pltpu
from jax.sharding import PartitionSpec as P

BLK = 128
SOFTENING = 0.5
UNROLL = 16
CHUNK = 32
VMEM_BYTES = 56 * 1024 * 1024
SLOPE = 1.1283737853323306
ERF_SERIES = (
    0.07159415430567773,
    -0.00022649025157034893,
    -0.000190667906232071,
    1.1875337467865749e-05,
)


def split3(values):
    high = values.astype(jnp.bfloat16).astype(jnp.float32)
    rest = values - high
    mid = rest.astype(jnp.bfloat16).astype(jnp.float32)
    low = (rest - mid).astype(jnp.bfloat16).astype(jnp.float32)
    return high, mid, low


def gather_kernel(place_ref, type_ref, krylov_ref, order_ref, geometry_ref, vectors_ref, stacked_ref):
    atoms = place_ref.shape[1]
    vecs = krylov_ref.shape[0]
    groups = atoms // BLK
    rows = 16 + vecs
    width = 2 * BLK
    together = 8
    high, mid, low = split3(place_ref[...])
    kinds = type_ref[...].astype(jnp.float32)
    empty = jnp.zeros((6, atoms), jnp.float32)
    full = jnp.concatenate([high, mid, low, kinds, empty, krylov_ref[...]], axis=0).astype(jnp.bfloat16)
    for group in range(groups):
        stacked_ref[group * rows : (group + 1) * rows] = full[:, group * BLK : (group + 1) * BLK]
    lane_ids = lax.broadcasted_iota(jnp.int32, (BLK, width), 0)

    def chunk_step(step, carry):
        lanes = pl.ds(pl.multiple_of(step * width, width), width)
        order = order_ref[:, lanes]
        picked = (lane_ids == order % BLK).astype(jnp.float32).astype(jnp.bfloat16)
        group_of = jnp.broadcast_to(order // BLK, (rows, width))
        total = jnp.zeros((rows, width), jnp.float32)
        for first in range(0, groups, together):
            here = jnp.dot(
                stacked_ref[first * rows : (first + together) * rows], picked, preferred_element_type=jnp.float32
            )
            for offset in range(together):
                part = here[offset * rows : (offset + 1) * rows]
                total = jnp.where(group_of == first + offset, part, total)
        place = total[0:3] + total[3:6] + total[6:9]
        geometry_ref[:, lanes] = jnp.concatenate([place, total[9:10]], axis=0)
        vectors_ref[:, lanes] = total[16:].astype(jnp.bfloat16)
        return carry

    lax.fori_loop(0, atoms // width, chunk_step, 0, unroll=2)


def gathered(positions, atom_type, krylov, order):
    vecs, atoms = krylov.shape
    vmem = pl.BlockSpec(memory_space=pltpu.VMEM)
    return pl.pallas_call(
        gather_kernel,
        in_specs=[vmem] * 4,
        out_specs=[vmem] * 2,
        out_shape=[
            jax.ShapeDtypeStruct((4, atoms), jnp.float32),
            jax.ShapeDtypeStruct((vecs, atoms), jnp.bfloat16),
        ],
        scratch_shapes=[pltpu.VMEM((atoms // BLK * (16 + vecs), BLK), jnp.bfloat16)],
        compiler_params=pltpu.CompilerParams(vmem_limit_bytes=VMEM_BYTES),
        cost_estimate=pl.CostEstimate(
            flops=2 * (16 + vecs) * atoms * atoms, bytes_accessed=8 * vecs * atoms, transcendentals=0
        ),
        name="gather_atoms",
    )(positions, atom_type[None, :], krylov, order[None, :])


def scatter_kernel(order_ref, krylov_ref, type_ref, hard_ref, valid_ref, *refs):
    parts, (out_ref, split_ref) = refs[:-2], refs[-2:]
    vecs, atoms = krylov_ref.shape
    groups = atoms // BLK
    chunk = 1024
    total = parts[0][...]
    for index, part in enumerate(parts[1:]):
        total = total + jnp.where(valid_ref[0, index] > 0, part[...].astype(jnp.float32), 0.0)
    high = total.astype(jnp.bfloat16).astype(jnp.float32)
    split_ref[0:vecs] = high
    split_ref[vecs:] = total - high

    lane_ids = lax.broadcasted_iota(jnp.int32, (BLK, chunk), 0)

    def chunk_step(step, total):
        lanes = pl.ds(pl.multiple_of(step * chunk, chunk), chunk)
        order = order_ref[:, lanes]
        group_of, lane_of = order // BLK, order % BLK
        placed = (lane_ids == lane_of).astype(jnp.float32).astype(jnp.bfloat16)
        values = split_ref[:, lanes]
        masked = jnp.concatenate(
            [jnp.where(group_of == group, values, 0.0).astype(jnp.bfloat16) for group in range(groups)], axis=0
        )
        return total + lax.dot_general(
            masked, placed, (((1,), (1,)), ((), ())), preferred_element_type=jnp.float32
        )

    moved = lax.fori_loop(
        0, atoms // chunk, chunk_step, jnp.zeros((groups * 2 * vecs, BLK), jnp.float32)
    )
    kinds = type_ref[...]
    hardness = jnp.zeros((1, atoms), jnp.float32)
    for kind in range(hard_ref.shape[0]):
        hardness = jnp.where(kinds == kind, hard_ref[kind], hardness)
    for group in range(groups):
        lanes = slice(group * BLK, (group + 1) * BLK)
        first = group * 2 * vecs
        placed = moved[first : first + vecs] + moved[first + vecs : first + 2 * vecs]
        out_ref[:, lanes] = placed + hardness[:, lanes] * krylov_ref[:, lanes]


def scattered(order, krylov, atom_type, type_hard, valid, parts):
    vecs, atoms = krylov.shape
    vmem = pl.BlockSpec(memory_space=pltpu.VMEM)
    return pl.pallas_call(
        scatter_kernel,
        in_specs=[vmem] * 3 + [pl.BlockSpec(memory_space=pltpu.SMEM)] * 2 + [vmem] * len(parts),
        out_specs=vmem,
        out_shape=jax.ShapeDtypeStruct((vecs, atoms), jnp.float32),
        scratch_shapes=[pltpu.VMEM((2 * vecs, atoms), jnp.float32)],
        compiler_params=pltpu.CompilerParams(vmem_limit_bytes=VMEM_BYTES),
        cost_estimate=pl.CostEstimate(
            flops=4 * vecs * atoms * atoms, bytes_accessed=24 * vecs * atoms, transcendentals=0
        ),
        name="scatter_atoms",
    )(order[None, :], krylov, atom_type[None, :], type_hard, valid, *parts)


def lanes_of(block):
    return pl.ds(pl.multiple_of(block * BLK, BLK), BLK)


def pair_kernel(slabs, left_blocks, left_ids, right_ids, count_ref, width_ref, *refs):
    geo_refs, vec_refs = refs[:slabs], refs[slabs : 2 * slabs]
    out_refs = refs[2 * slabs : 3 * slabs]
    left_ref, origin_ref, geo_ref, mix_ref, vec_ref, acc_ref, both_ref, tile_ref = refs[3 * slabs :]
    atoms = geo_refs[0].shape[1]
    blocks = slabs * atoms // BLK
    row_id = lax.broadcasted_iota(jnp.int32, (8, BLK), 0)
    type_width = jnp.ones((8, BLK), jnp.float32)
    for kind in range(width_ref.shape[0]):
        type_width = jnp.where(row_id == kind, width_ref[kind], type_width)
    geo_ref[4:8] = jnp.zeros((4, geo_ref.shape[1]), jnp.float32)

    for slab in range(slabs):
        geo_ref[0:4, slab * atoms : (slab + 1) * atoms] = geo_refs[slab][...]
        vec_ref[:, slab * atoms : (slab + 1) * atoms] = vec_refs[slab][...]
    acc_ref[...] = jnp.zeros_like(acc_ref)

    def one_hot(geometry):
        return jnp.where(row_id.astype(jnp.float32) == geometry[3:4, :], 1.0, 0.0)

    def mix_step(block, carry):
        hot = one_hot(geo_ref[:, lanes_of(block)])
        width = jnp.sum(hot * type_width, axis=0, keepdims=True)
        high, mid, low = split3(SLOPE * lax.rsqrt(type_width * type_width + width * width))
        mix_ref[:, lanes_of(block)] = jnp.concatenate([high, mid, low, jnp.zeros_like(low)], axis=0).astype(
            jnp.bfloat16
        )
        return carry

    lax.fori_loop(0, blocks, mix_step, 0, unroll=4)

    def left_step(block, carry):
        geometry = geo_ref[:, lanes_of(block)]
        hot = one_hot(geometry)
        origin = jnp.broadcast_to(geometry[:, 0:1], (8, BLK))
        origin_ref[block] = origin
        local = jnp.where(row_id < 3, geometry - origin, 0.0)
        norm = jnp.sum(local * local, axis=0, keepdims=True) + SOFTENING * SOFTENING
        side = jnp.where(row_id < 3, -2.0 * local, jnp.where(row_id == 3, 1.0, jnp.where(row_id == 4, norm, 0.0)))
        high, mid, low = split3(side)
        rows = jnp.concatenate(
            [high, high, mid, mid, high, low, hot, hot, hot, jnp.zeros((BLK - 72, BLK), jnp.float32)], axis=0
        )
        left_ref[block] = rows.T.astype(jnp.bfloat16)
        return carry

    lax.fori_loop(0, left_blocks, left_step, 0, unroll=4)

    both_ref[...] = jnp.ones_like(both_ref)
    tile_ref[...] = jnp.zeros_like(tile_ref)
    slots = left_ids.shape[1]
    live = count_ref[0]
    zero_side = jnp.zeros((48, BLK), jnp.bfloat16)
    zero_mix = jnp.zeros((32, BLK), jnp.bfloat16)
    zero_tail = jnp.zeros((BLK - 80, 2 * BLK), jnp.bfloat16)

    def weights_of(left, right):
        geometry = geo_ref[:, lanes_of(right)]
        local = jnp.where(row_id < 3, geometry - origin_ref[left], 0.0)
        norm = jnp.sum(local * local, axis=0, keepdims=True)
        side = jnp.where(row_id == 3, norm, jnp.where(row_id == 4, 1.0, local))
        high, mid, low = split3(side)
        rows = jnp.concatenate([high, mid, high, mid, low, high], axis=0).astype(jnp.bfloat16)
        mix = mix_ref[:, lanes_of(right)]
        return jnp.concatenate(
            [
                jnp.concatenate([rows, zero_side], axis=1),
                jnp.concatenate([zero_mix, mix], axis=1),
                zero_tail,
            ],
            axis=0,
        )

    def screened(square, inverse_width):
        inverse = lax.rsqrt(square)
        narrow = square * inverse * inverse_width
        power = narrow * narrow
        series = jnp.bfloat16(ERF_SERIES[-1])
        for factor in ERF_SERIES[-2::-1] + (1.0,):
            series = series * power + jnp.bfloat16(factor)
        return jnp.tanh(narrow * series) * inverse

    def slot_ids(turn, offset):
        slot = turn * UNROLL + offset
        place = jnp.clip(slot, 0, slots - 1)
        return left_ids[0, place], right_ids[0, place], (slot >= 0) & (slot < live)

    def pair_step(turn, carry):
        done = []
        for offset in range(UNROLL):
            left, right, alive = slot_ids(turn - 2, offset)
            tile = tile_ref[offset]
            forward = lax.dot_general(
                vec_ref[:, lanes_of(right)], tile, (((1,), (1,)), ((), ())), preferred_element_type=jnp.float32
            )
            backward = jnp.dot(vec_ref[:, lanes_of(left)], tile, preferred_element_type=jnp.float32)
            done.append((left, right, forward, backward, alive))
        for offset in range(UNROLL):
            for first in range(0, BLK, CHUNK):
                rows = slice(first, first + CHUNK)
                tile_ref[offset, rows] = screened(both_ref[offset, rows, :BLK], both_ref[offset, rows, BLK:])
        for offset in range(UNROLL):
            left, right, _ = slot_ids(turn, offset)
            both_ref[offset] = jnp.dot(
                left_ref[left], weights_of(left, right), preferred_element_type=jnp.float32
            ).astype(jnp.bfloat16)
        for left, right, forward, backward, alive in done:
            acc_ref[:, lanes_of(left)] += jnp.where(alive, forward, 0.0)
            acc_ref[:, lanes_of(right)] += jnp.where(alive & (left != right), backward, 0.0)
        return carry

    lax.fori_loop(0, (live + UNROLL - 1) // UNROLL + 2, pair_step, 0)

    for slab in range(slabs):
        out_refs[slab][...] = acc_ref[:, slab * atoms : (slab + 1) * atoms].astype(out_refs[slab].dtype)


def pair_sums(geometries, vectors, left_ids, right_ids, count, type_width, left_blocks):
    slabs = len(geometries)
    atoms = geometries[0].shape[1]
    vecs = vectors[0].shape[0]
    smem = pl.BlockSpec(memory_space=pltpu.SMEM)
    vmem = pl.BlockSpec(memory_space=pltpu.VMEM)
    kinds = [jnp.float32] + [jnp.bfloat16] * (slabs - 1)
    return pl.pallas_call(
        functools.partial(pair_kernel, slabs, left_blocks),
        in_specs=[smem] * 4 + [vmem] * (2 * slabs),
        out_specs=[vmem] * slabs,
        out_shape=[jax.ShapeDtypeStruct((vecs, atoms), kind) for kind in kinds],
        scratch_shapes=[
            pltpu.VMEM((left_blocks, BLK, BLK), jnp.bfloat16),
            pltpu.VMEM((left_blocks, 8, BLK), jnp.float32),
            pltpu.VMEM((8, slabs * atoms), jnp.float32),
            pltpu.VMEM((32, slabs * atoms), jnp.bfloat16),
            pltpu.VMEM((vecs, slabs * atoms), jnp.bfloat16),
            pltpu.VMEM((vecs, slabs * atoms), jnp.float32),
            pltpu.VMEM((UNROLL, BLK, 2 * BLK), jnp.bfloat16),
            pltpu.VMEM((UNROLL, BLK, BLK), jnp.bfloat16),
        ],
        compiler_params=pltpu.CompilerParams(vmem_limit_bytes=VMEM_BYTES),
        cost_estimate=pl.CostEstimate(
            flops=left_ids.shape[1] * BLK * BLK * (4 * vecs + 320),
            bytes_accessed=slabs * atoms * (32 + 4 * vecs),
            transcendentals=2 * left_ids.shape[1] * BLK * BLK,
        ),
        name="pair_sums",
    )(left_ids, right_ids, count, type_width, *geometries, *vectors)


def exchange_kernel(peers, toward, items, meanwhile, *refs):
    count = len(peers) * items
    sources = refs[:count]
    targets, (send_sems, recv_sems) = refs[-2 - count : -2], refs[-2:]
    barrier = pltpu.get_barrier_semaphore()

    def neighbour(axis, shift):
        size, here = lax.axis_size(axis), lax.axis_index(axis)
        there = here + shift
        if axis == "col":
            return {axis: lax.rem(there + size, size)}, there == there
        return {axis: there}, (there >= 0) & (there < size)

    expected = jnp.int32(0)
    for axis, step in peers:
        device, exists = neighbour(axis, -toward * step)

        @pl.when(exists)
        def _():
            pl.semaphore_signal(barrier, inc=1, device_id=device, device_id_type=pl.DeviceIdType.MESH)

        expected = expected + neighbour(axis, toward * step)[1].astype(jnp.int32)
    pl.semaphore_wait(barrier, expected)

    def copy_of(index):
        axis, step = peers[index // items]
        device, exists = neighbour(axis, toward * step)
        copy = pltpu.make_async_remote_copy(
            src_ref=sources[index],
            dst_ref=targets[index],
            send_sem=send_sems.at[index],
            recv_sem=recv_sems.at[index],
            device_id=device,
            device_id_type=pl.DeviceIdType.MESH,
        )
        return copy, exists, neighbour(axis, -toward * step)[1]

    for index in range(count):
        copy, exists, _ = copy_of(index)
        pl.when(exists)(copy.start)
    if meanwhile is not None:
        meanwhile(*refs[count : -2 - count])
    for index in range(count):
        copy, exists, arrives = copy_of(index)
        pl.when(exists)(copy.wait_send)
        pl.when(arrives)(copy.wait_recv)


def slot_ids_kernel(shard_blocks, peers, rows_ref, cols_ref, left_ref, right_ref, valid_ref):
    col_devices = lax.axis_size("col")
    rows, cols = rows_ref[...], cols_ref[...]
    row_slab = (rows // shard_blocks + (col_devices - lax.axis_index("col"))) % col_devices
    left_ref[...] = row_slab * shard_blocks + rows % shard_blocks
    step = jnp.clip(cols // shard_blocks - lax.axis_index("row"), 0, 2)
    right_slab = jnp.where(step == 0, 0, step + col_devices - 1)
    right_ref[...] = right_slab * shard_blocks + cols % shard_blocks
    place = lax.broadcasted_iota(jnp.int32, valid_ref.shape, 1)
    valid = jnp.ones(valid_ref.shape, jnp.int32)
    for index, (axis, shift) in enumerate(peers):
        if axis == "row":
            valid = jnp.where(place == index, (lax.axis_index("row") >= shift).astype(jnp.int32), valid)
    valid_ref[...] = valid


def exchanged(panels, peers, toward, collective_id, meanwhile=None, extras=(), extra_outs=()):
    items = len(panels[0])
    flat = [item for panel in panels for item in panel]
    vmem = pl.BlockSpec(memory_space=pltpu.VMEM)
    results = pl.pallas_call(
        functools.partial(exchange_kernel, peers, toward, items, meanwhile),
        in_specs=[pl.BlockSpec(memory_space=pl.ANY)] * len(flat) + [vmem] * len(extras),
        out_specs=[vmem] * len(extra_outs) + [pl.BlockSpec(memory_space=pl.ANY)] * len(flat),
        out_shape=list(extra_outs) + [jax.ShapeDtypeStruct(item.shape, item.dtype) for item in flat],
        scratch_shapes=[pltpu.SemaphoreType.DMA((len(flat),)), pltpu.SemaphoreType.DMA((len(flat),))],
        compiler_params=pltpu.CompilerParams(
            collective_id=collective_id, has_side_effects=True, vmem_limit_bytes=VMEM_BYTES
        ),
        name="send_atoms" if collective_id == 0 else "return_sums",
    )(*flat, *extras)
    moved = results[len(extra_outs) :]
    arrived = [moved[first : first + items] for first in range(0, len(flat), items)]
    return arrived, results[: len(extra_outs)]


def on_device(
    positions, atom_type, krylov, block_order, type_width, type_hard, pair_rows, pair_cols, pair_count
):
    vecs, atoms = krylov.shape
    shard_blocks = atoms // BLK
    geometry, vectors = gathered(positions, atom_type, krylov, block_order)

    col_devices = lax.axis_size("col")
    peers = [("col", step) for step in range(1, col_devices)] + [("row", 1), ("row", 2)]
    rows_list = pair_rows.reshape(1, -1)
    cols_list = pair_cols.reshape(1, -1)
    ids = jax.ShapeDtypeStruct(rows_list.shape, jnp.int32)
    arrived, (left_ids, right_ids, valid) = exchanged(
        [(geometry, vectors)] * len(peers),
        peers,
        -1,
        0,
        functools.partial(slot_ids_kernel, shard_blocks, peers),
        (rows_list, cols_list),
        (ids, ids, jax.ShapeDtypeStruct((1, BLK), jnp.int32)),
    )
    geometries = [geometry] + [panel[0] for panel in arrived]
    panels = [vectors] + [panel[1] for panel in arrived]
    sums = pair_sums(
        geometries, panels, left_ids, right_ids, pair_count.reshape(1), type_width, col_devices * shard_blocks
    )
    returned, _ = exchanged([(part,) for part in sums[1:]], peers, 1, 1)
    return scattered(block_order, krylov, atom_type, type_hard, valid, [sums[0]] + [panel[0] for panel in returned])


def solution(mesh):
    placed = (
        P(None, ("row", "col")),
        P(("row", "col")),
        P(None, ("row", "col")),
        P(("row", "col")),
        P(),
        P(),
        P("row", "col", None),
        P("row", "col", None),
        P("row", "col"),
    )
    return jax.shard_map(
        on_device, mesh=mesh, in_specs=placed, out_specs=P(None, ("row", "col")), check_vma=False
    )
```

```python
import functools

import jax
import jax.numpy as jnp
from jax import lax
from jax.experimental import pallas as pl
from jax.experimental.pallas import tpu as pltpu
from jax.sharding import PartitionSpec as P

BLK = 128
SOFTENING = 0.5
UNROLL = 16
CHUNK = 32
VMEM_BYTES = 56 * 1024 * 1024
SLOPE = 1.1283737853323306
ERF_SERIES = (
    0.07159415430567773,
    -0.00022649025157034893,
    -0.000190667906232071,
    1.1875337467865749e-05,
)


def split3(values):
    high = values.astype(jnp.bfloat16).astype(jnp.float32)
    rest = values - high
    mid = rest.astype(jnp.bfloat16).astype(jnp.float32)
    low = (rest - mid).astype(jnp.bfloat16).astype(jnp.float32)
    return high, mid, low


def gather_kernel(place_ref, type_ref, krylov_ref, order_ref, geometry_ref, vectors_ref, stacked_ref):
    atoms = place_ref.shape[1]
    vecs = krylov_ref.shape[0]
    groups = atoms // BLK
    rows = 16 + vecs
    width = 2 * BLK
    together = 8
    high, mid, low = split3(place_ref[...])
    kinds = type_ref[...].astype(jnp.float32)
    empty = jnp.zeros((6, atoms), jnp.float32)
    full = jnp.concatenate([high, mid, low, kinds, empty, krylov_ref[...]], axis=0).astype(jnp.bfloat16)
    for group in range(groups):
        stacked_ref[group * rows : (group + 1) * rows] = full[:, group * BLK : (group + 1) * BLK]
    lane_ids = lax.broadcasted_iota(jnp.int32, (BLK, width), 0)

    def chunk_step(step, carry):
        lanes = pl.ds(pl.multiple_of(step * width, width), width)
        order = order_ref[:, lanes]
        picked = (lane_ids == order % BLK).astype(jnp.float32).astype(jnp.bfloat16)
        group_of = jnp.broadcast_to(order // BLK, (rows, width))
        total = jnp.zeros((rows, width), jnp.float32)
        for first in range(0, groups, together):
            here = jnp.dot(
                stacked_ref[first * rows : (first + together) * rows], picked, preferred_element_type=jnp.float32
            )
            for offset in range(together):
                part = here[offset * rows : (offset + 1) * rows]
                total = jnp.where(group_of == first + offset, part, total)
        place = total[0:3] + total[3:6] + total[6:9]
        geometry_ref[:, lanes] = jnp.concatenate([place, total[9:10]], axis=0)
        vectors_ref[:, lanes] = total[16:].astype(jnp.bfloat16)
        return carry

    lax.fori_loop(0, atoms // width, chunk_step, 0, unroll=2)


def gathered(positions, atom_type, krylov, order):
    vecs, atoms = krylov.shape
    vmem = pl.BlockSpec(memory_space=pltpu.VMEM)
    return pl.pallas_call(
        gather_kernel,
        in_specs=[vmem] * 4,
        out_specs=[vmem] * 2,
        out_shape=[
            jax.ShapeDtypeStruct((4, atoms), jnp.float32),
            jax.ShapeDtypeStruct((vecs, atoms), jnp.bfloat16),
        ],
        scratch_shapes=[pltpu.VMEM((atoms // BLK * (16 + vecs), BLK), jnp.bfloat16)],
        compiler_params=pltpu.CompilerParams(vmem_limit_bytes=VMEM_BYTES),
        cost_estimate=pl.CostEstimate(
            flops=2 * (16 + vecs) * atoms * atoms, bytes_accessed=8 * vecs * atoms, transcendentals=0
        ),
        name="gather_atoms",
    )(positions, atom_type[None, :], krylov, order[None, :])


def scatter_kernel(order_ref, krylov_ref, type_ref, hard_ref, valid_ref, *refs):
    parts, (out_ref, split_ref) = refs[:-2], refs[-2:]
    vecs, atoms = krylov_ref.shape
    groups = atoms // BLK
    chunk = 1024
    total = parts[0][...]
    for index, part in enumerate(parts[1:]):
        total = total + jnp.where(valid_ref[0, index] > 0, part[...].astype(jnp.float32), 0.0)
    high = total.astype(jnp.bfloat16).astype(jnp.float32)
    split_ref[0:vecs] = high
    split_ref[vecs:] = total - high

    lane_ids = lax.broadcasted_iota(jnp.int32, (BLK, chunk), 0)

    def chunk_step(step, total):
        lanes = pl.ds(pl.multiple_of(step * chunk, chunk), chunk)
        order = order_ref[:, lanes]
        group_of, lane_of = order // BLK, order % BLK
        placed = (lane_ids == lane_of).astype(jnp.float32).astype(jnp.bfloat16)
        values = split_ref[:, lanes]
        masked = jnp.concatenate(
            [jnp.where(group_of == group, values, 0.0).astype(jnp.bfloat16) for group in range(groups)], axis=0
        )
        return total + lax.dot_general(
            masked, placed, (((1,), (1,)), ((), ())), preferred_element_type=jnp.float32
        )

    moved = lax.fori_loop(
        0, atoms // chunk, chunk_step, jnp.zeros((groups * 2 * vecs, BLK), jnp.float32)
    )
    kinds = type_ref[...]
    hardness = jnp.zeros((1, atoms), jnp.float32)
    for kind in range(hard_ref.shape[0]):
        hardness = jnp.where(kinds == kind, hard_ref[kind], hardness)
    for group in range(groups):
        lanes = slice(group * BLK, (group + 1) * BLK)
        first = group * 2 * vecs
        placed = moved[first : first + vecs] + moved[first + vecs : first + 2 * vecs]
        out_ref[:, lanes] = placed + hardness[:, lanes] * krylov_ref[:, lanes]


def scattered(order, krylov, atom_type, type_hard, valid, parts):
    vecs, atoms = krylov.shape
    vmem = pl.BlockSpec(memory_space=pltpu.VMEM)
    return pl.pallas_call(
        scatter_kernel,
        in_specs=[vmem] * 3 + [pl.BlockSpec(memory_space=pltpu.SMEM)] * 2 + [vmem] * len(parts),
        out_specs=vmem,
        out_shape=jax.ShapeDtypeStruct((vecs, atoms), jnp.float32),
        scratch_shapes=[pltpu.VMEM((2 * vecs, atoms), jnp.float32)],
        compiler_params=pltpu.CompilerParams(vmem_limit_bytes=VMEM_BYTES),
        cost_estimate=pl.CostEstimate(
            flops=4 * vecs * atoms * atoms, bytes_accessed=24 * vecs * atoms, transcendentals=0
        ),
        name="scatter_atoms",
    )(order[None, :], krylov, atom_type[None, :], type_hard, valid, *parts)


def lanes_of(block):
    return pl.ds(pl.multiple_of(block * BLK, BLK), BLK)


def pair_kernel(slabs, left_blocks, left_ids, right_ids, count_ref, width_ref, *refs):
    geo_refs, vec_refs = refs[:slabs], refs[slabs : 2 * slabs]
    out_refs = refs[2 * slabs : 3 * slabs]
    left_ref, origin_ref, geo_ref, mix_ref, vec_ref, acc_ref, both_ref, tile_ref = refs[3 * slabs :]
    atoms = geo_refs[0].shape[1]
    blocks = slabs * atoms // BLK
    row_id = lax.broadcasted_iota(jnp.int32, (8, BLK), 0)
    type_width = jnp.ones((8, BLK), jnp.float32)
    for kind in range(width_ref.shape[0]):
        type_width = jnp.where(row_id == kind, width_ref[kind], type_width)
    geo_ref[4:8] = jnp.zeros((4, geo_ref.shape[1]), jnp.float32)

    for slab in range(slabs):
        geo_ref[0:4, slab * atoms : (slab + 1) * atoms] = geo_refs[slab][...]
        vec_ref[:, slab * atoms : (slab + 1) * atoms] = vec_refs[slab][...]
    acc_ref[...] = jnp.zeros_like(acc_ref)

    def one_hot(geometry):
        return jnp.where(row_id.astype(jnp.float32) == geometry[3:4, :], 1.0, 0.0)

    def mix_step(block, carry):
        hot = one_hot(geo_ref[:, lanes_of(block)])
        width = jnp.sum(hot * type_width, axis=0, keepdims=True)
        high, mid, low = split3(SLOPE * lax.rsqrt(type_width * type_width + width * width))
        mix_ref[:, lanes_of(block)] = jnp.concatenate([high, mid, low, jnp.zeros_like(low)], axis=0).astype(
            jnp.bfloat16
        )
        return carry

    lax.fori_loop(0, blocks, mix_step, 0, unroll=4)

    def left_step(block, carry):
        geometry = geo_ref[:, lanes_of(block)]
        hot = one_hot(geometry)
        origin = jnp.broadcast_to(geometry[:, 0:1], (8, BLK))
        origin_ref[block] = origin
        local = jnp.where(row_id < 3, geometry - origin, 0.0)
        norm = jnp.sum(local * local, axis=0, keepdims=True) + SOFTENING * SOFTENING
        side = jnp.where(row_id < 3, -2.0 * local, jnp.where(row_id == 3, 1.0, jnp.where(row_id == 4, norm, 0.0)))
        high, mid, low = split3(side)
        rows = jnp.concatenate(
            [high, high, mid, mid, high, low, hot, hot, hot, jnp.zeros((BLK - 72, BLK), jnp.float32)], axis=0
        )
        left_ref[block] = rows.T.astype(jnp.bfloat16)
        return carry

    lax.fori_loop(0, left_blocks, left_step, 0, unroll=4)

    slots = left_ids.shape[1]
    live = count_ref[0]
    zero_side = jnp.zeros((48, BLK), jnp.bfloat16)
    zero_mix = jnp.zeros((32, BLK), jnp.bfloat16)
    zero_tail = jnp.zeros((BLK - 80, 2 * BLK), jnp.bfloat16)

    def weights_of(left, right):
        geometry = geo_ref[:, lanes_of(right)]
        local = jnp.where(row_id < 3, geometry - origin_ref[left], 0.0)
        norm = jnp.sum(local * local, axis=0, keepdims=True)
        side = jnp.where(row_id == 3, norm, jnp.where(row_id == 4, 1.0, local))
        high, mid, low = split3(side)
        rows = jnp.concatenate([high, mid, high, mid, low, high], axis=0).astype(jnp.bfloat16)
        mix = mix_ref[:, lanes_of(right)]
        return jnp.concatenate(
            [
                jnp.concatenate([rows, zero_side], axis=1),
                jnp.concatenate([zero_mix, mix], axis=1),
                zero_tail,
            ],
            axis=0,
        )

    def screened(square, inverse_width):
        inverse = lax.rsqrt(square)
        narrow = (square * inverse * inverse_width).astype(jnp.bfloat16)
        power = narrow * narrow
        series = jnp.bfloat16(ERF_SERIES[-1])
        for factor in ERF_SERIES[-2::-1] + (1.0,):
            series = series * power + jnp.bfloat16(factor)
        return jnp.tanh(narrow * series) * inverse.astype(jnp.bfloat16)

    def slot_ids(turn, offset):
        slot = turn * UNROLL + offset
        place = jnp.clip(slot, 0, slots - 1)
        return left_ids[0, place], right_ids[0, place], (slot >= 0) & (slot < live)

    def pair_step(turn, products=True, tiles=True, starts=True):
        done = []
        for offset in range(UNROLL if products else 0):
            left, right, alive = slot_ids(turn - 2, offset)
            tile = tile_ref[offset]
            forward = lax.dot_general(
                vec_ref[:, lanes_of(right)], tile, (((1,), (1,)), ((), ())), preferred_element_type=jnp.float32
            )
            backward = jnp.dot(vec_ref[:, lanes_of(left)], tile, preferred_element_type=jnp.float32)
            done.append((left, right, forward, backward, alive))
        for offset in range(UNROLL if tiles else 0):
            for first in range(0, BLK, CHUNK):
                rows = slice(first, first + CHUNK)
                tile_ref[offset, rows] = screened(both_ref[offset, rows, :BLK], both_ref[offset, rows, BLK:])
        for offset in range(UNROLL if starts else 0):
            left, right, _ = slot_ids(turn, offset)
            both_ref[offset] = jnp.dot(
                left_ref[left], weights_of(left, right), preferred_element_type=jnp.float32
            )
        for left, right, forward, backward, alive in done:
            acc_ref[:, lanes_of(left)] += jnp.where(alive, forward, 0.0)
            acc_ref[:, lanes_of(right)] += jnp.where(alive & (left != right), backward, 0.0)

    def full_step(turn, carry):
        pair_step(turn)
        return carry

    turns = jnp.maximum((live + UNROLL - 1) // UNROLL, 2)
    pair_step(0, products=False, tiles=False)
    pair_step(1, products=False)
    lax.fori_loop(2, turns, full_step, 0)
    pair_step(turns, starts=False)
    pair_step(turns + 1, tiles=False, starts=False)

    for slab in range(slabs):
        out_refs[slab][...] = acc_ref[:, slab * atoms : (slab + 1) * atoms].astype(out_refs[slab].dtype)


def pair_sums(geometries, vectors, left_ids, right_ids, count, type_width, left_blocks):
    slabs = len(geometries)
    atoms = geometries[0].shape[1]
    vecs = vectors[0].shape[0]
    smem = pl.BlockSpec(memory_space=pltpu.SMEM)
    vmem = pl.BlockSpec(memory_space=pltpu.VMEM)
    kinds = [jnp.float32] + [jnp.bfloat16] * (slabs - 1)
    return pl.pallas_call(
        functools.partial(pair_kernel, slabs, left_blocks),
        in_specs=[smem] * 4 + [vmem] * (2 * slabs),
        out_specs=[vmem] * slabs,
        out_shape=[jax.ShapeDtypeStruct((vecs, atoms), kind) for kind in kinds],
        scratch_shapes=[
            pltpu.VMEM((left_blocks, BLK, BLK), jnp.bfloat16),
            pltpu.VMEM((left_blocks, 8, BLK), jnp.float32),
            pltpu.VMEM((8, slabs * atoms), jnp.float32),
            pltpu.VMEM((32, slabs * atoms), jnp.bfloat16),
            pltpu.VMEM((vecs, slabs * atoms), jnp.bfloat16),
            pltpu.VMEM((vecs, slabs * atoms), jnp.float32),
            pltpu.VMEM((UNROLL, BLK, 2 * BLK), jnp.float32),
            pltpu.VMEM((UNROLL, BLK, BLK), jnp.bfloat16),
        ],
        compiler_params=pltpu.CompilerParams(vmem_limit_bytes=VMEM_BYTES),
        cost_estimate=pl.CostEstimate(
            flops=left_ids.shape[1] * BLK * BLK * (4 * vecs + 320),
            bytes_accessed=slabs * atoms * (32 + 4 * vecs),
            transcendentals=2 * left_ids.shape[1] * BLK * BLK,
        ),
        name="pair_sums",
    )(left_ids, right_ids, count, type_width, *geometries, *vectors)


def exchange_kernel(peers, toward, items, meanwhile, *refs):
    count = len(peers) * items
    sources = refs[:count]
    targets, (send_sems, recv_sems) = refs[-2 - count : -2], refs[-2:]
    barrier = pltpu.get_barrier_semaphore()

    def neighbour(axis, shift):
        size, here = lax.axis_size(axis), lax.axis_index(axis)
        there = here + shift
        if axis == "col":
            return {axis: lax.rem(there + size, size)}, there == there
        return {axis: there}, (there >= 0) & (there < size)

    expected = jnp.int32(0)
    for axis, step in peers:
        device, exists = neighbour(axis, -toward * step)

        @pl.when(exists)
        def _():
            pl.semaphore_signal(barrier, inc=1, device_id=device, device_id_type=pl.DeviceIdType.MESH)

        expected = expected + neighbour(axis, toward * step)[1].astype(jnp.int32)
    pl.semaphore_wait(barrier, expected)

    def copy_of(index):
        axis, step = peers[index // items]
        device, exists = neighbour(axis, toward * step)
        copy = pltpu.make_async_remote_copy(
            src_ref=sources[index],
            dst_ref=targets[index],
            send_sem=send_sems.at[index],
            recv_sem=recv_sems.at[index],
            device_id=device,
            device_id_type=pl.DeviceIdType.MESH,
        )
        return copy, exists, neighbour(axis, -toward * step)[1]

    for index in range(count):
        copy, exists, _ = copy_of(index)
        pl.when(exists)(copy.start)
    if meanwhile is not None:
        meanwhile(*refs[count : -2 - count])
    for index in range(count):
        copy, exists, arrives = copy_of(index)
        pl.when(exists)(copy.wait_send)
        pl.when(arrives)(copy.wait_recv)


def slot_ids_kernel(shard_blocks, peers, rows_ref, cols_ref, left_ref, right_ref, valid_ref):
    col_devices = lax.axis_size("col")
    rows, cols = rows_ref[...], cols_ref[...]
    row_slab = (rows // shard_blocks + (col_devices - lax.axis_index("col"))) % col_devices
    left_ref[...] = row_slab * shard_blocks + rows % shard_blocks
    step = jnp.clip(cols // shard_blocks - lax.axis_index("row"), 0, 2)
    right_slab = jnp.where(step == 0, 0, step + col_devices - 1)
    right_ref[...] = right_slab * shard_blocks + cols % shard_blocks
    place = lax.broadcasted_iota(jnp.int32, valid_ref.shape, 1)
    valid = jnp.ones(valid_ref.shape, jnp.int32)
    for index, (axis, shift) in enumerate(peers):
        if axis == "row":
            valid = jnp.where(place == index, (lax.axis_index("row") >= shift).astype(jnp.int32), valid)
    valid_ref[...] = valid


def exchanged(panels, peers, toward, collective_id, meanwhile=None, extras=(), extra_outs=()):
    items = len(panels[0])
    flat = [item for panel in panels for item in panel]
    vmem = pl.BlockSpec(memory_space=pltpu.VMEM)
    results = pl.pallas_call(
        functools.partial(exchange_kernel, peers, toward, items, meanwhile),
        in_specs=[pl.BlockSpec(memory_space=pl.ANY)] * len(flat) + [vmem] * len(extras),
        out_specs=[vmem] * len(extra_outs) + [pl.BlockSpec(memory_space=pl.ANY)] * len(flat),
        out_shape=list(extra_outs) + [jax.ShapeDtypeStruct(item.shape, item.dtype) for item in flat],
        scratch_shapes=[pltpu.SemaphoreType.DMA((len(flat),)), pltpu.SemaphoreType.DMA((len(flat),))],
        compiler_params=pltpu.CompilerParams(
            collective_id=collective_id, has_side_effects=True, vmem_limit_bytes=VMEM_BYTES
        ),
        name="send_atoms" if collective_id == 0 else "return_sums",
    )(*flat, *extras)
    moved = results[len(extra_outs) :]
    arrived = [moved[first : first + items] for first in range(0, len(flat), items)]
    return arrived, results[: len(extra_outs)]


def on_device(
    positions, atom_type, krylov, block_order, type_width, type_hard, pair_rows, pair_cols, pair_count
):
    vecs, atoms = krylov.shape
    shard_blocks = atoms // BLK
    geometry, vectors = gathered(positions, atom_type, krylov, block_order)

    col_devices = lax.axis_size("col")
    peers = [("col", step) for step in range(1, col_devices)] + [("row", 1), ("row", 2)]
    rows_list = pair_rows.reshape(1, -1)
    cols_list = pair_cols.reshape(1, -1)
    ids = jax.ShapeDtypeStruct(rows_list.shape, jnp.int32)
    arrived, (left_ids, right_ids, valid) = exchanged(
        [(geometry, vectors)] * len(peers),
        peers,
        -1,
        0,
        functools.partial(slot_ids_kernel, shard_blocks, peers),
        (rows_list, cols_list),
        (ids, ids, jax.ShapeDtypeStruct((1, BLK), jnp.int32)),
    )
    geometries = [geometry] + [panel[0] for panel in arrived]
    panels = [vectors] + [panel[1] for panel in arrived]
    sums = pair_sums(
        geometries, panels, left_ids, right_ids, pair_count.reshape(1), type_width, col_devices * shard_blocks
    )
    returned, _ = exchanged([(part,) for part in sums[1:]], peers, 1, 1)
    return scattered(block_order, krylov, atom_type, type_hard, valid, [sums[0]] + [panel[0] for panel in returned])


def solution(mesh):
    placed = (
        P(None, ("row", "col")),
        P(("row", "col")),
        P(None, ("row", "col")),
        P(("row", "col")),
        P(),
        P(),
        P("row", "col", None),
        P("row", "col", None),
        P("row", "col"),
    )
    return jax.shard_map(
        on_device, mesh=mesh, in_specs=placed, out_specs=P(None, ("row", "col")), check_vma=False
    )
```

```python
import functools

import jax
import jax.numpy as jnp
from jax import lax
from jax.experimental import pallas as pl
from jax.experimental.pallas import tpu as pltpu
from jax.sharding import PartitionSpec as P

BLK = 128
SOFTENING = 0.5
UNROLL = 16
CHUNK = 32
VMEM_BYTES = 56 * 1024 * 1024
SLOPE = 1.1283737853323306
ERF_SERIES = (
    0.07159415430567773,
    -0.00022649025157034893,
    -0.000190667906232071,
    1.1875337467865749e-05,
)


def split3(values):
    high = values.astype(jnp.bfloat16).astype(jnp.float32)
    rest = values - high
    mid = rest.astype(jnp.bfloat16).astype(jnp.float32)
    low = (rest - mid).astype(jnp.bfloat16).astype(jnp.float32)
    return high, mid, low


def gather_kernel(place_ref, type_ref, krylov_ref, order_ref, geometry_ref, vectors_ref, stacked_ref):
    atoms = place_ref.shape[1]
    vecs = krylov_ref.shape[0]
    groups = atoms // BLK
    rows = 16 + vecs
    width = 2 * BLK
    together = 8
    high, mid, low = split3(place_ref[...])
    kinds = type_ref[...].astype(jnp.float32)
    empty = jnp.zeros((6, atoms), jnp.float32)
    full = jnp.concatenate([high, mid, low, kinds, empty, krylov_ref[...]], axis=0).astype(jnp.bfloat16)
    for group in range(groups):
        stacked_ref[group * rows : (group + 1) * rows] = full[:, group * BLK : (group + 1) * BLK]
    lane_ids = lax.broadcasted_iota(jnp.int32, (BLK, width), 0)

    def chunk_step(step, carry):
        lanes = pl.ds(pl.multiple_of(step * width, width), width)
        order = order_ref[:, lanes]
        picked = (lane_ids == order % BLK).astype(jnp.float32).astype(jnp.bfloat16)
        group_of = jnp.broadcast_to(order // BLK, (rows, width))
        total = jnp.zeros((rows, width), jnp.float32)
        for first in range(0, groups, together):
            here = jnp.dot(
                stacked_ref[first * rows : (first + together) * rows], picked, preferred_element_type=jnp.float32
            )
            for offset in range(together):
                part = here[offset * rows : (offset + 1) * rows]
                total = jnp.where(group_of == first + offset, part, total)
        place = total[0:3] + total[3:6] + total[6:9]
        geometry_ref[:, lanes] = jnp.concatenate([place, total[9:10]], axis=0)
        vectors_ref[:, lanes] = total[16:].astype(jnp.bfloat16)
        return carry

    lax.fori_loop(0, atoms // width, chunk_step, 0, unroll=2)


def gathered(positions, atom_type, krylov, order):
    vecs, atoms = krylov.shape
    vmem = pl.BlockSpec(memory_space=pltpu.VMEM)
    return pl.pallas_call(
        gather_kernel,
        in_specs=[vmem] * 4,
        out_specs=[vmem] * 2,
        out_shape=[
            jax.ShapeDtypeStruct((4, atoms), jnp.float32),
            jax.ShapeDtypeStruct((vecs, atoms), jnp.bfloat16),
        ],
        scratch_shapes=[pltpu.VMEM((atoms // BLK * (16 + vecs), BLK), jnp.bfloat16)],
        compiler_params=pltpu.CompilerParams(vmem_limit_bytes=VMEM_BYTES),
        cost_estimate=pl.CostEstimate(
            flops=2 * (16 + vecs) * atoms * atoms, bytes_accessed=8 * vecs * atoms, transcendentals=0
        ),
        name="gather_atoms",
    )(positions, atom_type[None, :], krylov, order[None, :])


def scatter_kernel(order_ref, krylov_ref, type_ref, hard_ref, valid_ref, *refs):
    parts, (out_ref, split_ref) = refs[:-2], refs[-2:]
    vecs, atoms = krylov_ref.shape
    groups = atoms // BLK
    chunk = 1024
    total = parts[0][...]
    for index, part in enumerate(parts[1:]):
        total = total + jnp.where(valid_ref[0, index] > 0, part[...].astype(jnp.float32), 0.0)
    high = total.astype(jnp.bfloat16).astype(jnp.float32)
    split_ref[0:vecs] = high
    split_ref[vecs:] = total - high

    lane_ids = lax.broadcasted_iota(jnp.int32, (BLK, chunk), 0)

    def chunk_step(step, total):
        lanes = pl.ds(pl.multiple_of(step * chunk, chunk), chunk)
        order = order_ref[:, lanes]
        group_of, lane_of = order // BLK, order % BLK
        placed = (lane_ids == lane_of).astype(jnp.float32).astype(jnp.bfloat16)
        values = split_ref[:, lanes]
        masked = jnp.concatenate(
            [jnp.where(group_of == group, values, 0.0).astype(jnp.bfloat16) for group in range(groups)], axis=0
        )
        return total + lax.dot_general(
            masked, placed, (((1,), (1,)), ((), ())), preferred_element_type=jnp.float32
        )

    moved = lax.fori_loop(
        0, atoms // chunk, chunk_step, jnp.zeros((groups * 2 * vecs, BLK), jnp.float32)
    )
    kinds = type_ref[...]
    hardness = jnp.zeros((1, atoms), jnp.float32)
    for kind in range(hard_ref.shape[0]):
        hardness = jnp.where(kinds == kind, hard_ref[kind], hardness)
    for group in range(groups):
        lanes = slice(group * BLK, (group + 1) * BLK)
        first = group * 2 * vecs
        placed = moved[first : first + vecs] + moved[first + vecs : first + 2 * vecs]
        out_ref[:, lanes] = placed + hardness[:, lanes] * krylov_ref[:, lanes]


def scattered(order, krylov, atom_type, type_hard, valid, parts):
    vecs, atoms = krylov.shape
    vmem = pl.BlockSpec(memory_space=pltpu.VMEM)
    return pl.pallas_call(
        scatter_kernel,
        in_specs=[vmem] * 3 + [pl.BlockSpec(memory_space=pltpu.SMEM)] * 2 + [vmem] * len(parts),
        out_specs=vmem,
        out_shape=jax.ShapeDtypeStruct((vecs, atoms), jnp.float32),
        scratch_shapes=[pltpu.VMEM((2 * vecs, atoms), jnp.float32)],
        compiler_params=pltpu.CompilerParams(vmem_limit_bytes=VMEM_BYTES),
        cost_estimate=pl.CostEstimate(
            flops=4 * vecs * atoms * atoms, bytes_accessed=24 * vecs * atoms, transcendentals=0
        ),
        name="scatter_atoms",
    )(order[None, :], krylov, atom_type[None, :], type_hard, valid, *parts)


def lanes_of(block):
    return pl.ds(pl.multiple_of(block * BLK, BLK), BLK)


def pair_kernel(slabs, left_blocks, left_ids, right_ids, count_ref, width_ref, *refs):
    geo_refs, vec_refs = refs[:slabs], refs[slabs : 2 * slabs]
    out_refs = refs[2 * slabs : 3 * slabs]
    left_ref, origin_ref, geo_ref, mix_ref, vec_ref, acc_ref, both_ref, tile_ref = refs[3 * slabs :]
    atoms = geo_refs[0].shape[1]
    blocks = slabs * atoms // BLK
    row_id = lax.broadcasted_iota(jnp.int32, (8, BLK), 0)
    type_width = jnp.ones((8, BLK), jnp.float32)
    for kind in range(width_ref.shape[0]):
        type_width = jnp.where(row_id == kind, width_ref[kind], type_width)
    geo_ref[4:8] = jnp.zeros((4, geo_ref.shape[1]), jnp.float32)

    for slab in range(slabs):
        geo_ref[0:4, slab * atoms : (slab + 1) * atoms] = geo_refs[slab][...]
        vec_ref[:, slab * atoms : (slab + 1) * atoms] = vec_refs[slab][...]
    acc_ref[...] = jnp.zeros_like(acc_ref)

    def one_hot(geometry):
        return jnp.where(row_id.astype(jnp.float32) == geometry[3:4, :], 1.0, 0.0)

    def mix_step(block, carry):
        hot = one_hot(geo_ref[:, lanes_of(block)])
        width = jnp.sum(hot * type_width, axis=0, keepdims=True)
        high, mid, low = split3(SLOPE * lax.rsqrt(type_width * type_width + width * width))
        mix_ref[:, lanes_of(block)] = jnp.concatenate([high, mid, low, jnp.zeros_like(low)], axis=0).astype(
            jnp.bfloat16
        )
        return carry

    lax.fori_loop(0, blocks, mix_step, 0, unroll=4)

    def left_step(block, carry):
        geometry = geo_ref[:, lanes_of(block)]
        hot = one_hot(geometry)
        origin = jnp.broadcast_to(geometry[:, 0:1], (8, BLK))
        origin_ref[block] = origin
        local = jnp.where(row_id < 3, geometry - origin, 0.0)
        norm = jnp.sum(local * local, axis=0, keepdims=True) + SOFTENING * SOFTENING
        side = jnp.where(row_id < 3, -2.0 * local, jnp.where(row_id == 3, 1.0, jnp.where(row_id == 4, norm, 0.0)))
        high, mid, low = split3(side)
        rows = jnp.concatenate(
            [high, high, mid, mid, high, low, hot, hot, hot, jnp.zeros((BLK - 72, BLK), jnp.float32)], axis=0
        )
        left_ref[block] = rows.T.astype(jnp.bfloat16)
        return carry

    lax.fori_loop(0, left_blocks, left_step, 0, unroll=4)

    slots = left_ids.shape[1]
    live = count_ref[0]
    zero_side = jnp.zeros((48, BLK), jnp.bfloat16)
    zero_mix = jnp.zeros((32, BLK), jnp.bfloat16)
    zero_tail = jnp.zeros((BLK - 80, 2 * BLK), jnp.bfloat16)

    def weights_of(left, right):
        geometry = geo_ref[:, lanes_of(right)]
        local = jnp.where(row_id < 3, geometry - origin_ref[left], 0.0)
        norm = jnp.sum(local * local, axis=0, keepdims=True)
        side = jnp.where(row_id == 3, norm, jnp.where(row_id == 4, 1.0, local))
        high, mid, low = split3(side)
        rows = jnp.concatenate([high, mid, high, mid, low, high], axis=0).astype(jnp.bfloat16)
        mix = mix_ref[:, lanes_of(right)]
        return jnp.concatenate(
            [
                jnp.concatenate([rows, zero_side], axis=1),
                jnp.concatenate([zero_mix, mix], axis=1),
                zero_tail,
            ],
            axis=0,
        )

    def screened(square, inverse_width):
        inverse = lax.rsqrt(square)
        narrow = (square * inverse * inverse_width).astype(jnp.bfloat16)
        power = narrow * narrow
        series = jnp.bfloat16(ERF_SERIES[-1])
        for factor in ERF_SERIES[-2::-1] + (1.0,):
            series = series * power + jnp.bfloat16(factor)
        return jnp.tanh(narrow * series) * inverse.astype(jnp.bfloat16)

    def slot_ids(turn, offset):
        slot = turn * UNROLL + offset
        place = jnp.clip(slot, 0, slots - 1)
        return left_ids[0, place], right_ids[0, place], (slot >= 0) & (slot < live)

    def pair_step(turn, products=True, tiles=True, starts=True):
        done = []
        for offset in range(UNROLL if products else 0):
            left, right, alive = slot_ids(turn - 2, offset)
            tile = tile_ref[offset]
            forward = lax.dot_general(
                vec_ref[:, lanes_of(right)], tile, (((1,), (1,)), ((), ())), preferred_element_type=jnp.float32
            )
            backward = jnp.dot(vec_ref[:, lanes_of(left)], tile, preferred_element_type=jnp.float32)
            done.append((left, right, forward, backward, alive))
        for offset in range(UNROLL if tiles else 0):
            for first in range(0, BLK, CHUNK):
                rows = slice(first, first + CHUNK)
                tile_ref[offset, rows] = screened(both_ref[offset, rows, :BLK], both_ref[offset, rows, BLK:])
        for offset in range(UNROLL if starts else 0):
            left, right, _ = slot_ids(turn, offset)
            both_ref[offset] = jnp.dot(
                left_ref[left], weights_of(left, right), preferred_element_type=jnp.float32
            )
        for left, right, forward, backward, alive in done:
            acc_ref[:, lanes_of(left)] += jnp.where(alive, forward, 0.0)
            acc_ref[:, lanes_of(right)] += jnp.where(alive & (left != right), backward, 0.0)

    def full_step(turn, carry):
        pair_step(turn)
        return carry

    turns = jnp.maximum((live + UNROLL - 1) // UNROLL, 2)
    pair_step(0, products=False, tiles=False)
    pair_step(1, products=False)
    lax.fori_loop(2, turns, full_step, 0)
    pair_step(turns, starts=False)
    pair_step(turns + 1, tiles=False, starts=False)

    for slab in range(slabs):
        out_refs[slab][...] = acc_ref[:, slab * atoms : (slab + 1) * atoms].astype(out_refs[slab].dtype)


def pair_sums(geometries, vectors, left_ids, right_ids, count, type_width, left_blocks):
    slabs = len(geometries)
    atoms = geometries[0].shape[1]
    vecs = vectors[0].shape[0]
    smem = pl.BlockSpec(memory_space=pltpu.SMEM)
    vmem = pl.BlockSpec(memory_space=pltpu.VMEM)
    kinds = [jnp.float32] + [jnp.bfloat16] * (slabs - 1)
    return pl.pallas_call(
        functools.partial(pair_kernel, slabs, left_blocks),
        in_specs=[smem] * 4 + [vmem] * (2 * slabs),
        out_specs=[vmem] * slabs,
        out_shape=[jax.ShapeDtypeStruct((vecs, atoms), kind) for kind in kinds],
        scratch_shapes=[
            pltpu.VMEM((left_blocks, BLK, BLK), jnp.bfloat16),
            pltpu.VMEM((left_blocks, 8, BLK), jnp.float32),
            pltpu.VMEM((8, slabs * atoms), jnp.float32),
            pltpu.VMEM((32, slabs * atoms), jnp.bfloat16),
            pltpu.VMEM((vecs, slabs * atoms), jnp.bfloat16),
            pltpu.VMEM((vecs, slabs * atoms), jnp.float32),
            pltpu.VMEM((UNROLL, BLK, 2 * BLK), jnp.float32),
            pltpu.VMEM((UNROLL, BLK, BLK), jnp.bfloat16),
        ],
        compiler_params=pltpu.CompilerParams(vmem_limit_bytes=VMEM_BYTES),
        cost_estimate=pl.CostEstimate(
            flops=left_ids.shape[1] * BLK * BLK * (4 * vecs + 320),
            bytes_accessed=slabs * atoms * (32 + 4 * vecs),
            transcendentals=2 * left_ids.shape[1] * BLK * BLK,
        ),
        name="pair_sums",
    )(left_ids, right_ids, count, type_width, *geometries, *vectors)


def exchange_kernel(peers, toward, items, meanwhile, relay, *refs):
    count = len(peers) * items
    sources = refs[:count]
    targets, (send_sems, recv_sems) = refs[-2 - count : -2], refs[-2:]
    barrier = pltpu.get_barrier_semaphore()

    def neighbour(axis, shift):
        size, here = lax.axis_size(axis), lax.axis_index(axis)
        there = here + shift
        if axis == "col":
            return {axis: lax.rem(there + size, size)}, there == there
        return {axis: there}, (there >= 0) & (there < size)

    rows, row = lax.axis_size("row"), lax.axis_index("row")
    even = lax.rem(row, 2) == 0
    arriving = row + 2 < rows

    def receiver(axis, step):
        if relay and (axis, step) == ("row", 1):
            return {axis: jnp.where(even, row + 1, row - 1)}, jnp.logical_not(even) | arriving
        return neighbour(axis, toward * step)

    def sender(axis, step):
        if relay and (axis, step) == ("row", 1):
            return {axis: jnp.where(even, row + 1, row - 1)}, even | (row + 1 < rows)
        return neighbour(axis, -toward * step)

    expected = jnp.int32(0)
    for axis, step in peers:
        device, exists = sender(axis, step)

        @pl.when(exists)
        def _():
            pl.semaphore_signal(barrier, inc=1, device_id=device, device_id_type=pl.DeviceIdType.MESH)

        expected = expected + receiver(axis, step)[1].astype(jnp.int32)
    pl.semaphore_wait(barrier, expected)

    def copy_of(index, source=None):
        device, exists = receiver(*peers[index // items])
        copy = pltpu.make_async_remote_copy(
            src_ref=sources[index] if source is None else source,
            dst_ref=targets[index],
            send_sem=send_sems.at[index],
            recv_sem=recv_sems.at[index],
            device_id=device,
            device_id_type=pl.DeviceIdType.MESH,
        )
        return copy, exists, sender(*peers[index // items])[1]

    relayed = [index for index in range(count) if relay and peers[index // items] == ("row", 1)]
    for index in reversed(range(count)):
        copy, exists, _ = copy_of(index)
        pl.when(exists & jnp.logical_not(even) if index in relayed else exists)(copy.start)
    if meanwhile is not None:
        meanwhile(*refs[count : -2 - count])
    for index in relayed:
        first, _, arrives = copy_of(index + items)

        @pl.when(arrives)
        def _():
            first.wait_recv()

        onward, _, _ = copy_of(index, targets[index + items])
        pl.when(even & arriving)(onward.start)
    for index in range(count):
        copy, exists, arrives = copy_of(index)
        pl.when(exists)(copy.wait_send)
        if index - items not in relayed:
            pl.when(arrives)(copy.wait_recv)


def slot_ids_kernel(shard_blocks, peers, rows_ref, cols_ref, left_ref, right_ref, valid_ref):
    col_devices = lax.axis_size("col")
    rows, cols = rows_ref[...], cols_ref[...]
    row_slab = (rows // shard_blocks + (col_devices - lax.axis_index("col"))) % col_devices
    left_ref[...] = row_slab * shard_blocks + rows % shard_blocks
    step = jnp.clip(cols // shard_blocks - lax.axis_index("row"), 0, 2)
    right_slab = jnp.where(step == 0, 0, step + col_devices - 1)
    right_ref[...] = right_slab * shard_blocks + cols % shard_blocks
    place = lax.broadcasted_iota(jnp.int32, valid_ref.shape, 1)
    valid = jnp.ones(valid_ref.shape, jnp.int32)
    for index, (axis, shift) in enumerate(peers):
        if axis == "row":
            valid = jnp.where(place == index, (lax.axis_index("row") >= shift).astype(jnp.int32), valid)
    valid_ref[...] = valid


def exchanged(panels, peers, toward, collective_id, meanwhile=None, extras=(), extra_outs=(), relay=False):
    items = len(panels[0])
    flat = [item for panel in panels for item in panel]
    vmem = pl.BlockSpec(memory_space=pltpu.VMEM)
    results = pl.pallas_call(
        functools.partial(exchange_kernel, peers, toward, items, meanwhile, relay),
        in_specs=[pl.BlockSpec(memory_space=pl.ANY)] * len(flat) + [vmem] * len(extras),
        out_specs=[vmem] * len(extra_outs) + [pl.BlockSpec(memory_space=pl.ANY)] * len(flat),
        out_shape=list(extra_outs) + [jax.ShapeDtypeStruct(item.shape, item.dtype) for item in flat],
        scratch_shapes=[pltpu.SemaphoreType.DMA((len(flat),)), pltpu.SemaphoreType.DMA((len(flat),))],
        compiler_params=pltpu.CompilerParams(
            collective_id=collective_id, has_side_effects=True, vmem_limit_bytes=VMEM_BYTES
        ),
        name="send_atoms" if collective_id == 0 else "return_sums",
    )(*flat, *extras)
    moved = results[len(extra_outs) :]
    arrived = [moved[first : first + items] for first in range(0, len(flat), items)]
    return arrived, results[: len(extra_outs)]


def on_device(
    positions, atom_type, krylov, block_order, type_width, type_hard, pair_rows, pair_cols, pair_count
):
    vecs, atoms = krylov.shape
    shard_blocks = atoms // BLK
    geometry, vectors = gathered(positions, atom_type, krylov, block_order)

    col_devices = lax.axis_size("col")
    peers = [("col", step) for step in range(1, col_devices)] + [("row", 1), ("row", 2)]
    rows_list = pair_rows.reshape(1, -1)
    cols_list = pair_cols.reshape(1, -1)
    ids = jax.ShapeDtypeStruct(rows_list.shape, jnp.int32)
    arrived, (left_ids, right_ids, valid) = exchanged(
        [(geometry, vectors)] * len(peers),
        peers,
        -1,
        0,
        functools.partial(slot_ids_kernel, shard_blocks, peers),
        (rows_list, cols_list),
        (ids, ids, jax.ShapeDtypeStruct((1, BLK), jnp.int32)),
        relay=lax.axis_size("row") % 2 == 0,
    )
    geometries = [geometry] + [panel[0] for panel in arrived]
    panels = [vectors] + [panel[1] for panel in arrived]
    sums = pair_sums(
        geometries, panels, left_ids, right_ids, pair_count.reshape(1), type_width, col_devices * shard_blocks
    )
    returned, _ = exchanged([(part,) for part in sums[1:]], peers, 1, 1)
    return scattered(block_order, krylov, atom_type, type_hard, valid, [sums[0]] + [panel[0] for panel in returned])


def solution(mesh):
    placed = (
        P(None, ("row", "col")),
        P(("row", "col")),
        P(None, ("row", "col")),
        P(("row", "col")),
        P(),
        P(),
        P("row", "col", None),
        P("row", "col", None),
        P("row", "col"),
    )
    return jax.shard_map(
        on_device, mesh=mesh, in_specs=placed, out_specs=P(None, ("row", "col")), check_vma=False
    )
```
